512 devices in a mesh: seq: 64 (over z, y), head: 8 (over x, core).
Axes of the slice: x: 4, y: 4, z: 16, core: 2. Of those that a mesh axis runs over, the one named last changes fastest.
Arguments:
- queries: bfloat16 [8192, 4096], P('seq', 'head'), may hold values from -6 to 6
- key_rows: bfloat16 [8192, 4096], P('seq', 'head'), may hold values from -6 to 6
- values: bfloat16 [8192, 4096], P('seq', 'head'), may hold values from -32 to 32
- cotangent: bfloat16 [8192, 4096], P(('seq', 'head')), may hold values from -6 to 6
- norm_gain: float32 [4096], replicated, may hold values from 0.5 to 2
Outputs:
- grad_queries: bfloat16 [8192, 4096], P('seq', 'head')
- grad_keys: bfloat16 [8192, 4096], P('seq', 'head')
- grad_values: bfloat16 [8192, 4096], P('seq', 'head')
The draws below stay inside these ranges and needn't reach their ends.
All inputs are finite; a program needn't handle non-finite values.
Results may differ from the reference program's by a relative error of at most 0.006.
Values may be sent and summed in bfloat16 or wider, within the bound.
A program may use at most 128 MiB of HBM per device.

```python
import math
import jax
import jax.numpy as jnp
from jax import lax

HEADS = 32
DH = 128
TOK_DEV = 128
D = 4096
TOKENS = 8192
N_SEQ = 64


def draw_values(key, part):
    key = jax.random.fold_in(key, 11)
    column_key = jax.random.fold_in(key, 0)
    entry_key = jax.random.fold_in(key, 2)
    column_scale = jnp.exp(jax.random.uniform(column_key, (1, D), jnp.float32, 0.0, math.log(10.0)))
    entries = jnp.clip(jax.random.normal(entry_key, (TOKENS, D), jnp.float32), -6.0, 6.0)
    return (entries * column_scale / 3.0).astype(jnp.bfloat16)


def shard_levels(own_key, shape, pieces, least, top_value):
    level = 1.0
    for dim, shards_of in pieces:
        draws = jax.random.uniform(jax.random.fold_in(jax.random.fold_in(own_key, 6), dim), (shards_of,), jnp.float32, least / len(pieces), top_value / len(pieces))
        level = level * jnp.repeat(jnp.exp(draws), shape[dim] // shards_of).reshape((-1,) + (1,) * (len(shape) - 1 - dim))
    return level


def normal_values(key, shape, spread, bound, shards=(), kind=jnp.bfloat16):
    drawn = jax.random.normal(key, shape, jnp.float32) * spread
    if len(shards) > 0:
        drawn = shard_levels(key, shape, shards, -0.22, 0.18) * drawn
    return jnp.clip(drawn, min=-bound, max=bound).astype(kind)


def setup_inputs(seed: int = 0) -> dict:
    key_list = jax.random.split(jax.random.key(seed), 6)
    return {
        "queries": normal_values(key_list[0], (TOKENS, D), 1.0, 6.0, ((0, 64), (1, 8))),
        "key_rows": normal_values(key_list[1], (TOKENS, D), 1.0, 6.0, ((0, 64), (1, 8))),
        "values": draw_values(jax.random.fold_in(key_list[5], 71), 0),
        "cotangent": normal_values(key_list[3], (TOKENS, D), 1.0, 6.0, ((0, 512),)),
        "norm_gain": jnp.clip(jnp.exp(jax.random.uniform(key_list[4], (D,), jnp.float32, math.log(0.5), math.log(2.0))), 0.5, 2.0),
    }


EPSILON = 1e-06

def rounded(array):
    return lax.optimization_barrier(array.astype(jnp.bfloat16)).astype(jnp.float32)

def split_heads(array):
    return array.reshape(N_SEQ, TOK_DEV, HEADS, DH).transpose(2, 0, 1, 3)

def join_heads(array):
    return array.transpose(1, 2, 0, 3).reshape(TOKENS, D)

def causal_mask():
    return jnp.arange(TOK_DEV)[:, None] >= jnp.arange(TOK_DEV)[None, :]

def forward_head(operands):
    scaling = DH ** (-0.5)
    query_wide = operands[0].astype(jnp.float32)
    key_wide = operands[1].astype(jnp.float32)
    value_wide = operands[2].astype(jnp.float32)
    states = jnp.einsum('btd,bte->bde', key_wide, value_wide)
    running = jnp.cumsum(states, axis=0)
    prefix = jnp.concatenate([jnp.zeros_like(states[:1]), running[:-1]], axis=0)
    prefix_round = rounded(prefix)
    scores = jnp.einsum('btd,bsd->bts', query_wide, key_wide) * scaling
    scores = rounded(jnp.where(causal_mask()[None], scores, jnp.float32(0.0)))
    inner = jnp.einsum('bts,bse->bte', scores, value_wide)
    outer = jnp.einsum('btd,bde->bte', query_wide, prefix_round) * scaling
    return ((inner + outer).astype(jnp.bfloat16), prefix_round)

def backward_head(operands):
    scaling = DH ** (-0.5)
    query_wide = operands[0].astype(jnp.float32)
    key_wide = operands[1].astype(jnp.float32)
    value_wide = operands[2].astype(jnp.float32)
    grad_wide = operands[3].astype(jnp.float32)
    prefix_round = operands[4]
    mask_full = causal_mask()[None]
    scores = jnp.einsum('btd,bsd->bts', query_wide, key_wide) * scaling
    scores = rounded(jnp.where(mask_full, scores, jnp.float32(0.0)))
    grad_states = jnp.einsum('btd,bte->bde', query_wide, grad_wide)
    running = jnp.cumsum(grad_states[::-1], axis=0)[::-1]
    suffix = jnp.concatenate([running[1:], jnp.zeros_like(grad_states[:1])], axis=0)
    suffix_round = rounded(suffix)
    grad_scores = jnp.einsum('bte,bse->bts', grad_wide, value_wide) * scaling
    grad_scores = rounded(jnp.where(mask_full, grad_scores, jnp.float32(0.0)))
    grad_query = jnp.einsum('bts,bsd->btd', grad_scores, key_wide)
    grad_query = grad_query + jnp.einsum('bte,bde->btd', grad_wide, prefix_round) * scaling
    grad_key = jnp.einsum('bts,btd->bsd', grad_scores, query_wide)
    grad_key = grad_key + jnp.einsum('bse,bde->bsd', value_wide, suffix_round) * scaling
    grad_value = jnp.einsum('bts,bte->bse', scores, grad_wide)
    grad_value = grad_value + jnp.einsum('bsd,bde->bse', key_wide, suffix_round) * scaling
    return (grad_query.astype(jnp.bfloat16), grad_key.astype(jnp.bfloat16), grad_value.astype(jnp.bfloat16))

def reference(queries, key_rows, values, cotangent, norm_gain):
    query_heads = split_heads(queries)
    key_heads = split_heads(key_rows)
    value_heads = split_heads(values)
    attended_heads, prefixes = lax.map(forward_head, (query_heads, key_heads, value_heads))
    attended = join_heads(attended_heads)
    wide = attended.astype(jnp.float32)
    inverse = lax.rsqrt(lax.optimization_barrier(jnp.mean(wide * wide, axis=1, keepdims=True)) + EPSILON)
    scaled_cot = cotangent.astype(jnp.float32) * norm_gain[None, :]
    cross = lax.optimization_barrier(jnp.mean(scaled_cot * wide, axis=1, keepdims=True))
    grad_attended = (inverse * scaled_cot - inverse * inverse * inverse * cross * wide).astype(jnp.bfloat16)
    grad_heads = split_heads(grad_attended)
    grad_query, grad_key, grad_value = lax.map(backward_head, (query_heads, key_heads, value_heads, grad_heads, prefixes))
    return (join_heads(grad_query), join_heads(grad_key), join_heads(grad_value))
```

```python
import functools

import jax
import jax.numpy as jnp
from jax import lax
from jax.experimental import pallas as pl
from jax.experimental.pallas import tpu as pltpu
from jax.sharding import PartitionSpec as P

DH = 128
EPSILON = 1e-06
GROUP = 16
HALVES = 2
CORES = 2
MESH = pl.DeviceIdType.MESH
F32 = jnp.float32
BF16 = jnp.bfloat16


def dot(left, right, left_dim, right_dim):
    dims = (((left_dim,), (right_dim,)), ((), ()))
    return lax.dot_general(left, right, dims, preferred_element_type=F32)


def remote(src, dst, send_sem, recv_sem, seq, head):
    return pltpu.make_async_remote_copy(
        src_ref=src,
        dst_ref=dst,
        send_sem=send_sem,
        recv_sem=recv_sem,
        device_id=(seq, head),
        device_id_type=MESH,
    )


def wait_bytes(ref, sem):
    pltpu.make_async_copy(ref, ref, sem).wait()


class Scan:
    def __init__(self, place, backward, state, inbox, part, total, total_in, offset, back, out, sems):
        self.seq, self.head, self.group, self.me, self.size, self.groups = place
        self.backward = backward
        self.state, self.inbox, self.part, self.total = state, inbox, part, total
        self.total_in, self.offset, self.back, self.out = total_in, offset, back, out
        self.s1, self.r1, self.s2, self.r2, self.s3, self.r3 = sems
        self.rows = inbox.shape[2]
        self.core = lax.rem(self.head, CORES)
        self.owner_head = self.head - self.core + CORES - 1
        self.owns = self.core == CORES - 1
        self.row = self.size // 4
        self.mine = self.piece(self.me, self.group)

    def slice_of(self, ref, owner):
        return ref.at[pl.ds(pl.multiple_of(owner * self.rows, self.rows), self.rows)]

    def piece(self, member, group):
        shifted = lax.rem((group + 1) // 2, 2)
        return lax.rem(member + shifted * (self.size // 2), self.size)

    def far_first(self, body):
        here, column = self.me // self.row, lax.rem(self.me, self.row)
        rows = self.size // self.row
        for other in (rows - 1 - here, lax.rem(here + 2, rows), here + 1 - 2 * lax.rem(here, 2), here):
            for step in range(1, self.row + (other is not here)):
                body(other * self.row + lax.rem(column + step, self.row))

    def to_owner(self, owner):
        return remote(
            self.slice_of(self.state, self.piece(owner, self.group)),
            self.inbox.at[self.core, self.me],
            self.s1,
            self.r1.at[self.core],
            self.group * self.size + owner,
            self.owner_head,
        )

    def to_group(self, core, distance, group):
        return remote(
            self.total.at[core],
            self.total_in.at[core, distance - 1],
            self.s2.at[core, distance - 1],
            self.r2.at[core, distance - 1],
            group * self.size + self.piece(self.mine, group),
            self.head,
        )

    def to_member(self, core, member):
        return remote(
            self.back.at[core, member],
            self.slice_of(self.out, self.mine),
            self.s3.at[core],
            self.r3,
            self.group * self.size + member,
            self.head - (CORES - 1) + core,
        )

    def groups_later(self, body):
        for distance in range(1, self.groups):
            if self.backward:
                group, there = self.group - distance, self.group >= distance
            else:
                group, there = self.group + distance, self.group + distance < self.groups
            pl.when(there)(functools.partial(body, distance, group))

    def groups_earlier(self, body):
        for distance in range(1, self.groups):
            if self.backward:
                there = self.group + distance < self.groups
            else:
                there = self.group >= distance
            pl.when(there)(functools.partial(body, distance))

    def by_core(self, first, second):
        pl.when(self.core != CORES - 1)(first)
        pl.when(self.owns)(second)

    def send_state(self):
        self.far_first(lambda owner: self.to_owner(owner).start())

        def keep():
            self.inbox[CORES - 1, self.me] = self.slice_of(self.state, self.mine)[...]

        self.by_core(lambda: self.to_owner(self.me).start(), keep)

    def sum_up(self, core):
        received = self.size - (core == CORES - 1)
        wait_bytes(self.inbox.at[core, pl.ds(0, received)], self.r1.at[core])
        running = jnp.zeros(self.offset.shape[1:], F32)
        order = range(self.size)
        for member in reversed(order) if self.backward else order:
            self.part[core, member] = running
            running = running + self.inbox[core, member].astype(F32)
        self.total[core] = running.astype(BF16)
        self.groups_later(lambda distance, group: self.to_group(core, distance, group).start())
        self.offset[core] = jnp.zeros(self.offset.shape[1:], F32)

    def answer(self, core):
        def add(distance):
            self.to_group(core, distance, self.group).wait_recv()
            self.offset[core] += self.total_in[core, distance - 1].astype(F32)

        self.groups_earlier(add)
        self.back[core] = (self.offset[core][None] + self.part[core]).astype(BF16)
        self.far_first(lambda member: self.to_member(core, member).start())
        if core == CORES - 1:
            self.slice_of(self.out, self.mine)[...] = self.back[core, self.me]
        else:
            self.to_member(core, self.me).start()

    def receive(self):
        def wait(count):
            wait_bytes(self.back.at[0, pl.ds(0, count)], self.r3)

        self.by_core(lambda: wait(self.size), lambda: wait(self.size - 1))

    def drain(self):
        def sent(count):
            wait_bytes(self.inbox.at[0, pl.ds(0, count)], self.s1)

        def owner_sent():
            sent(self.size - 1)
            for core in range(CORES):
                self.groups_later(lambda distance, group: self.to_group(core, distance, group).wait_send())
                wait_bytes(self.back.at[core, pl.ds(0, self.size - (core == CORES - 1))], self.s3.at[core])

        self.by_core(lambda: sent(self.size), owner_sent)


def kernel(n_seq, n_head, size, *refs):
    q_hbm, k_hbm, v_hbm, cot_hbm, gain_hbm, gq, gk, gv = refs[:8]
    q, k, v, cot, gain, cot_block, scaled, inner, scores_t, query_t = refs[8:18]
    attended, grad, key_part, value_part, stat, stat_in = refs[18:24]
    local_sems, cot_send, cot_recv, stat_send, stat_recv = refs[24:29]
    scan_refs = [refs[at : at + 14] for at in range(29, 29 + 14 * 2 * HALVES, 14)]

    seq, head = lax.axis_index("seq"), lax.axis_index("head")
    groups = n_seq // size
    group, me = seq // size, lax.rem(seq, size)
    tokens, width = q.shape
    heads = width // DH
    cot_rows = cot.shape[0]
    scaling = DH ** (-0.5)
    place = (seq, head, group, me, size, groups)
    scans = [Scan(place, i >= HALVES, *own[:8], own[8:]) for i, own in enumerate(scan_refs)]
    forward, backward = scans[:HALVES], scans[HALVES:]
    columns = [slice(h * DH, (h + 1) * DH) for h in range(heads)]
    part_heads = heads // HALVES
    halves = [range(i * part_heads, (i + 1) * part_heads) for i in range(HALVES)]

    loads = [
        pltpu.make_async_copy(src, dst, local_sems.at[i])
        for i, (src, dst) in enumerate(
            [(k_hbm, k), (v_hbm, v), (cot_hbm, cot), (q_hbm, q), (gain_hbm, gain)]
        )
    ]
    for load in loads[:2]:
        load.start()

    barrier = pltpu.get_barrier_semaphore()

    def greet(other_seq, other_head):
        pl.semaphore_signal(
            barrier, inc=1, device_id=(other_seq, other_head), device_id_type=MESH
        )

    def greet_owners():
        forward[0].far_first(lambda member: greet(group * size + member, head + 1))

    def greet_owned():
        for step in range(1, groups):
            other = lax.rem(group + step, groups)
            greet(other * size + forward[0].piece(forward[0].mine, other), head)
        forward[0].far_first(lambda member: greet(group * size + member, head - 1))
        forward[0].far_first(lambda member: greet(group * size + member, head))

    forward[0].by_core(greet_owners, greet_owned)
    for step in range(1, n_head):
        greet(seq, lax.rem(head + step, n_head))
    for load in loads[2:]:
        load.start()

    loads[0].wait()
    loads[1].wait()
    for i, half in enumerate(halves):
        for h in half:
            state = dot(k[:, columns[h]], v[:, columns[h]], 0, 0)
            forward[i].state[columns[h - half[0]], :] = state.astype(BF16)
        if i == 0:
            forward[0].by_core(
                lambda: pl.semaphore_wait(barrier, size - 1 + n_head - 1),
                lambda: pl.semaphore_wait(barrier, 2 * (size - 1) + groups - 1 + n_head - 1),
            )
        forward[i].send_state()

    def cot_columns(to):
        return pl.ds(pl.multiple_of(to * width, width), width)

    def cot_rows_of(owner):
        return cot_block.at[pl.ds(pl.multiple_of(owner * cot_rows, cot_rows), cot_rows)]

    def cot_copy(to, owner):
        return remote(
            cot.at[:, cot_columns(to)],
            cot_rows_of(owner),
            cot_send,
            cot_recv,
            seq,
            to,
        )

    def over_heads(body):
        for step in range(1, n_head):
            body(lax.rem(head + step, n_head))

    loads[2].wait()
    over_heads(lambda to: cot_copy(to, head).start())
    cot_rows_of(head)[...] = cot[:, cot_columns(head)]

    loads[3].wait()
    loads[4].wait()
    rows = lax.broadcasted_iota(jnp.int32, (tokens, tokens), 0)
    cols = lax.broadcasted_iota(jnp.int32, (tokens, tokens), 1)

    def own_block(some):
        for h in some:
            qh, kh, vh = (ref[:, columns[h]] for ref in (q, k, v))
            raw = dot(qh, kh, 1, 1) * scaling
            masked = jnp.where(rows >= cols, raw, 0.0).astype(BF16)
            inner[:, columns[h]] = dot(masked, vh, 1, 0)

    def turned(some):
        for h in some:
            qh, kh = q[:, columns[h]], k[:, columns[h]]
            raw = dot(kh, qh, 1, 1) * scaling
            scores_t[h] = jnp.where(cols >= rows, raw, 0.0).astype(BF16)
            query_t[h] = qh.T

    own_block(halves[0])

    def each(step, some):
        def owner():
            for scan in some:
                for core in range(CORES):
                    step(scan, core)

        pl.when(some[0].owns)(owner)

    each(Scan.sum_up, forward)
    own_block(halves[1])
    wait_bytes(cot.at[:, pl.ds(0, (n_head - 1) * width)], cot_recv)
    scaled[...] = cot_block[...].astype(F32) * gain[:, cot_columns(head)]

    each(Scan.answer, forward)

    turned(range(heads))

    squares = jnp.zeros((tokens, DH), F32)
    products = jnp.zeros((tokens, DH), F32)
    for i, half in enumerate(halves):
        forward[i].receive()
        for h in half:
            prefix = forward[i].out[columns[h - half[0]], :]
            outer = dot(q[:, columns[h]], prefix, 1, 0) * scaling
            rounded = (inner[:, columns[h]] + outer).astype(BF16)
            attended[:, columns[h]] = rounded
            wide = rounded.astype(F32)
            squares = squares + wide * wide
            products = products + wide * scaled[:, columns[h]]
    square_row = jnp.sum(squares.T, axis=0, keepdims=True)
    product_row = jnp.sum(products.T, axis=0, keepdims=True)
    stat_rows = lax.broadcasted_iota(jnp.int32, stat.shape, 0)
    stat[...] = jnp.where(stat_rows == 0, square_row, product_row)

    def stat_copy(to, owner):
        return remote(
            stat, stat_in.at[owner], stat_send, stat_recv, seq, to
        )

    over_heads(lambda to: stat_copy(to, head).start())
    stat_in[head] = stat[...]
    wait_bytes(stat_in.at[pl.ds(0, n_head - 1)], stat_recv)
    summed = jnp.sum(stat_in[...], axis=0) * (1.0 / (n_head * width))
    inverse = lax.rsqrt(summed[0:1, :] + EPSILON)
    slope = inverse * inverse * inverse * summed[1:2, :]
    inverse = jnp.broadcast_to(inverse, (DH, tokens)).T
    slope = jnp.broadcast_to(slope, (DH, tokens)).T

    for i, half in enumerate(halves):
        for h in half:
            wide = attended[:, columns[h]].astype(F32)
            rounded = (inverse * scaled[:, columns[h]] - slope * wide).astype(BF16)
            grad[:, columns[h]] = rounded
            state = dot(query_t[h], rounded, 1, 0)
            backward[i].state[columns[h - half[0]], :] = state.astype(BF16)
        backward[i].send_state()

    def own_grads(h):
        at = columns[h]
        prefix = forward[h // part_heads].out[columns[h % part_heads], :]
        gh, qh, kh, vh = (ref[:, at] for ref in (grad, q, k, v))
        raw = dot(gh, vh, 1, 1) * scaling
        masked = jnp.where(rows >= cols, raw, 0.0).astype(BF16)
        raw = dot(vh, gh, 1, 1) * scaling
        masked_t = jnp.where(cols >= rows, raw, 0.0).astype(BF16)
        outer = dot(gh, prefix, 1, 1) * scaling
        gq[:, at] = (dot(masked, kh, 1, 0) + outer).astype(BF16)
        key_part[:, at] = dot(masked_t, qh, 1, 0)
        value_part[:, at] = dot(scores_t[h], gh, 1, 0)

    for h in range(heads - 2):
        own_grads(h)
    each(Scan.sum_up, backward)
    own_grads(heads - 2)
    each(Scan.answer, backward)
    own_grads(heads - 1)
    for i, half in enumerate(halves):
        backward[i].receive()
        for h in half:
            suffix = backward[i].out[columns[h - half[0]], :]
            outer = dot(v[:, columns[h]], suffix, 1, 1) * scaling
            gk[:, columns[h]] = (key_part[:, columns[h]] + outer).astype(BF16)
            outer = dot(k[:, columns[h]], suffix, 1, 0) * scaling
            gv[:, columns[h]] = (value_part[:, columns[h]] + outer).astype(BF16)

    for scan in scans:
        scan.drain()
    wait_bytes(cot.at[:, pl.ds(0, (n_head - 1) * width)], cot_send)
    wait_bytes(stat_in.at[pl.ds(0, n_head - 1)], stat_send)


def write_out(*refs):
    copies = [pltpu.make_async_copy(refs[i], refs[3 + i], refs[6].at[i]) for i in range(3)]
    for copy in copies:
        copy.start()
    for copy in copies:
        copy.wait()


def solution(mesh):
    n_seq, n_head = mesh.shape["seq"], mesh.shape["head"]
    size = GROUP
    groups = n_seq // size

    def local(queries, key_rows, values, cotangent, norm_gain):
        tokens, width = queries.shape
        heads = width // DH
        part = heads * DH // HALVES
        rows = part // size
        block = pltpu.VMEM((tokens, width), BF16)
        wide = pltpu.VMEM((tokens, width), F32)
        square = pltpu.VMEM((heads, DH, DH), BF16)
        scan = [
            pltpu.VMEM((part, DH), BF16),
            pltpu.VMEM((CORES, size, rows, DH), BF16),
            pltpu.VMEM((CORES, size, rows, DH), F32),
            pltpu.VMEM((CORES, rows, DH), BF16),
            pltpu.VMEM((CORES, groups - 1, rows, DH), BF16),
            pltpu.VMEM((CORES, rows, DH), F32),
            pltpu.VMEM((CORES, size, rows, DH), BF16),
            pltpu.VMEM((part, DH), BF16),
        ]
        dma = pltpu.SemaphoreType.DMA
        scan_sems = [dma, dma((CORES,))] + [dma((CORES, groups - 1))] * 2 + [dma((CORES,)), dma]
        out = pltpu.VMEM((tokens, width), BF16)
        grads = pl.pallas_call(
            functools.partial(kernel, n_seq, n_head, size),
            out_shape=(out, out, out),
            in_specs=[pl.BlockSpec(memory_space=pltpu.HBM)] * 5,
            out_specs=[pl.BlockSpec(memory_space=pltpu.VMEM)] * 3,
            scratch_shapes=[
                block,
                block,
                block,
                pltpu.VMEM(cotangent.shape, BF16),
                pltpu.VMEM((1, norm_gain.shape[0]), F32),
                block,
                wide,
                wide,
                square,
                square,
                block,
                block,
                wide,
                wide,
                pltpu.VMEM((8, tokens), F32),
                pltpu.VMEM((n_head, 8, tokens), F32),
                dma((5,)),
                dma,
                dma,
                dma,
                dma,
                *((scan + scan_sems) * (2 * HALVES)),
            ],
            compiler_params=pltpu.CompilerParams(
                collective_id=0, has_side_effects=True, vmem_limit_bytes=60 * 1024 * 1024
            ),
            cost_estimate=pl.CostEstimate(
                flops=26 * heads * DH**3, bytes_accessed=14 * tokens * width, transcendentals=0
            ),
        )(queries, key_rows, values, cotangent, norm_gain.reshape(1, -1))
        result = jax.ShapeDtypeStruct((tokens, width), BF16)
        return pl.pallas_call(
            write_out,
            out_shape=(result,) * 3,
            in_specs=[pl.BlockSpec(memory_space=pltpu.VMEM)] * 3,
            out_specs=[pl.BlockSpec(memory_space=pltpu.HBM)] * 3,
            scratch_shapes=[dma((3,))],
            compiler_params=pltpu.CompilerParams(vmem_limit_bytes=2 * 1024 * 1024),
        )(*grads)

    return jax.shard_map(
        local,
        mesh=mesh,
        in_specs=(P("seq", "head"), P("seq", "head"), P("seq", "head"), P(("seq", "head"), None), P()),
        out_specs=(P("seq", "head"), P("seq", "head"), P("seq", "head")),
        check_vma=False,
    )
```

```python
import functools

import jax
import jax.numpy as jnp
from jax import lax
from jax.experimental import pallas as pl
from jax.experimental.pallas import tpu as pltpu
from jax.sharding import PartitionSpec as P

DH = 128
EPSILON = 1e-06
GROUP = 16
HALVES = 1
CORES = 2
MESH = pl.DeviceIdType.MESH
F32 = jnp.float32
BF16 = jnp.bfloat16


def dot(left, right, left_dim, right_dim):
    dims = (((left_dim,), (right_dim,)), ((), ()))
    return lax.dot_general(left, right, dims, preferred_element_type=F32)


def remote(src, dst, send_sem, recv_sem, seq, head):
    return pltpu.make_async_remote_copy(
        src_ref=src,
        dst_ref=dst,
        send_sem=send_sem,
        recv_sem=recv_sem,
        device_id=(seq, head),
        device_id_type=MESH,
    )


def wait_bytes(ref, sem):
    pltpu.make_async_copy(ref, ref, sem).wait()


class Scan:
    def __init__(self, place, backward, state, inbox, part, total, total_in, offset, back, out, sems):
        self.seq, self.head, self.group, self.me, self.size, self.groups = place
        self.backward = backward
        self.state, self.inbox, self.part, self.total = state, inbox, part, total
        self.total_in, self.offset, self.back, self.out = total_in, offset, back, out
        self.s1, self.r1, self.s2, self.r2, self.s3, self.r3 = sems
        self.rows = inbox.shape[2]
        self.core = lax.rem(self.head, CORES)
        self.owner_head = self.head - self.core + CORES - 1
        self.owns = self.core == CORES - 1
        self.row = self.size // 4
        self.mine = self.piece(self.me, self.group)

    def slice_of(self, ref, owner):
        return ref.at[pl.ds(pl.multiple_of(owner * self.rows, self.rows), self.rows)]

    def piece(self, member, group):
        shifted = lax.rem((group + 1) // 2, 2)
        return lax.rem(member + shifted * (self.size // 2), self.size)

    def far_first(self, body, planes=slice(None)):
        here, column = self.me // self.row, lax.rem(self.me, self.row)
        rows = self.size // self.row
        others = (rows - 1 - here, lax.rem(here + 2, rows), here + 1 - 2 * lax.rem(here, 2), here)
        for other in others[planes]:
            for step in range(1, self.row + (other is not here)):
                body(other * self.row + lax.rem(column + step, self.row))

    def to_owner(self, owner):
        return remote(
            self.slice_of(self.state, self.piece(owner, self.group)),
            self.inbox.at[self.core, self.me],
            self.s1,
            self.r1.at[self.core],
            self.group * self.size + owner,
            self.owner_head,
        )

    def to_group(self, core, distance, group):
        return remote(
            self.total.at[core],
            self.total_in.at[core, distance - 1],
            self.s2.at[core, distance - 1],
            self.r2.at[core, distance - 1],
            group * self.size + self.piece(self.mine, group),
            self.head,
        )

    def to_member(self, core, member):
        return remote(
            self.back.at[core, member],
            self.slice_of(self.out, self.mine),
            self.s3.at[core],
            self.r3,
            self.group * self.size + member,
            self.head - (CORES - 1) + core,
        )

    def groups_later(self, body):
        for distance in range(1, self.groups):
            if self.backward:
                group, there = self.group - distance, self.group >= distance
            else:
                group, there = self.group + distance, self.group + distance < self.groups
            pl.when(there)(functools.partial(body, distance, group))

    def groups_earlier(self, body):
        for distance in range(1, self.groups):
            if self.backward:
                there = self.group + distance < self.groups
            else:
                there = self.group >= distance
            pl.when(there)(functools.partial(body, distance))

    def by_core(self, first, second):
        pl.when(self.core != CORES - 1)(first)
        pl.when(self.owns)(second)

    def send_state(self):
        self.far_first(lambda owner: self.to_owner(owner).start())

        def keep():
            self.inbox[CORES - 1, self.me] = self.slice_of(self.state, self.mine)[...]

        self.by_core(lambda: self.to_owner(self.me).start(), keep)

    def sum_up(self, core):
        received = self.size - (core == CORES - 1)
        wait_bytes(self.inbox.at[core, pl.ds(0, received)], self.r1.at[core])
        running = jnp.zeros(self.offset.shape[1:], F32)
        order = range(self.size)
        for member in reversed(order) if self.backward else order:
            self.part[core, member] = running
            running = running + self.inbox[core, member].astype(F32)
        self.total[core] = running.astype(BF16)
        self.groups_later(lambda distance, group: self.to_group(core, distance, group).start())
        self.offset[core] = jnp.zeros(self.offset.shape[1:], F32)

    def near(self, core):
        self.far_first(lambda member: self.to_member(core, member).start(), slice(2, 4))
        if core == CORES - 1:
            self.slice_of(self.out, self.mine)[...] = self.back[core, self.me]
        else:
            self.to_member(core, self.me).start()

    def answer(self, core):
        def add(distance):
            self.to_group(core, distance, self.group).wait_recv()
            self.offset[core] += self.total_in[core, distance - 1].astype(F32)

        self.groups_earlier(add)
        self.back[core] = (self.offset[core][None] + self.part[core]).astype(BF16)
        self.far_first(lambda member: self.to_member(core, member).start(), slice(0, 2))

    def receive(self):
        def wait(count):
            wait_bytes(self.back.at[0, pl.ds(0, count)], self.r3)

        self.by_core(lambda: wait(self.size), lambda: wait(self.size - 1))

    def drain(self):
        def sent(count):
            wait_bytes(self.inbox.at[0, pl.ds(0, count)], self.s1)

        def owner_sent():
            sent(self.size - 1)
            for core in range(CORES):
                self.groups_later(lambda distance, group: self.to_group(core, distance, group).wait_send())
                wait_bytes(self.back.at[core, pl.ds(0, self.size - (core == CORES - 1))], self.s3.at[core])

        self.by_core(lambda: sent(self.size), owner_sent)


def kernel(n_seq, n_head, size, *refs):
    q_hbm, k_hbm, v_hbm, cot_hbm, gain_hbm, gq, gk, gv = refs[:8]
    q, k, v, cot, gain, cot_block, scaled, inner, scores_t, query_t = refs[8:18]
    attended, grad, key_part, value_part, stat, stat_in = refs[18:24]
    local_sems, cot_send, cot_recv, stat_send, stat_recv = refs[24:29]
    scan_refs = [refs[at : at + 14] for at in range(29, 29 + 14 * 2 * HALVES, 14)]

    seq, head = lax.axis_index("seq"), lax.axis_index("head")
    groups = n_seq // size
    group, me = seq // size, lax.rem(seq, size)
    tokens, width = q.shape
    heads = width // DH
    cot_rows = cot.shape[0]
    scaling = DH ** (-0.5)
    place = (seq, head, group, me, size, groups)
    scans = [Scan(place, i >= HALVES, *own[:8], own[8:]) for i, own in enumerate(scan_refs)]
    forward, backward = scans[:HALVES], scans[HALVES:]
    columns = [slice(h * DH, (h + 1) * DH) for h in range(heads)]
    part_heads = heads // HALVES
    halves = [range(i * part_heads, (i + 1) * part_heads) for i in range(HALVES)]

    loads = [
        pltpu.make_async_copy(src, dst, local_sems.at[i])
        for i, (src, dst) in enumerate(
            [(k_hbm, k), (v_hbm, v), (cot_hbm, cot), (q_hbm, q), (gain_hbm, gain)]
        )
    ]
    for load in loads[:2]:
        load.start()

    barrier = pltpu.get_barrier_semaphore()

    def greet(other_seq, other_head):
        pl.semaphore_signal(
            barrier, inc=1, device_id=(other_seq, other_head), device_id_type=MESH
        )

    def greet_owners():
        forward[0].far_first(lambda member: greet(group * size + member, head + 1))

    def greet_owned():
        for step in range(1, groups):
            other = lax.rem(group + step, groups)
            greet(other * size + forward[0].piece(forward[0].mine, other), head)
        forward[0].far_first(lambda member: greet(group * size + member, head - 1))
        forward[0].far_first(lambda member: greet(group * size + member, head))

    forward[0].by_core(greet_owners, greet_owned)
    for step in range(1, n_head):
        greet(seq, lax.rem(head + step, n_head))
    for load in loads[2:]:
        load.start()

    loads[0].wait()
    loads[1].wait()
    for i, half in enumerate(halves):
        for h in half:
            state = dot(k[:, columns[h]], v[:, columns[h]], 0, 0)
            forward[i].state[columns[h - half[0]], :] = state.astype(BF16)
        if i == 0:
            forward[0].by_core(
                lambda: pl.semaphore_wait(barrier, size - 1 + n_head - 1),
                lambda: pl.semaphore_wait(barrier, 2 * (size - 1) + groups - 1 + n_head - 1),
            )
        forward[i].send_state()

    def cot_columns(to):
        return pl.ds(pl.multiple_of(to * width, width), width)

    def cot_rows_of(owner):
        return cot_block.at[pl.ds(pl.multiple_of(owner * cot_rows, cot_rows), cot_rows)]

    def cot_copy(to, owner):
        return remote(
            cot.at[:, cot_columns(to)],
            cot_rows_of(owner),
            cot_send,
            cot_recv,
            seq,
            to,
        )

    def over_heads(body):
        for step in range(1, n_head):
            body(lax.rem(head + step, n_head))

    loads[2].wait()
    over_heads(lambda to: cot_copy(to, head).start())
    cot_rows_of(head)[...] = cot[:, cot_columns(head)]

    loads[3].wait()
    loads[4].wait()
    rows = lax.broadcasted_iota(jnp.int32, (tokens, tokens), 0)
    cols = lax.broadcasted_iota(jnp.int32, (tokens, tokens), 1)

    def own_block(some):
        for h in some:
            qh, kh, vh = (ref[:, columns[h]] for ref in (q, k, v))
            raw = dot(qh, kh, 1, 1) * scaling
            masked = jnp.where(rows >= cols, raw, 0.0).astype(BF16)
            inner[:, columns[h]] = dot(masked, vh, 1, 0)

    def turned(some):
        for h in some:
            qh, kh = q[:, columns[h]], k[:, columns[h]]
            raw = dot(kh, qh, 1, 1) * scaling
            scores_t[h] = jnp.where(cols >= rows, raw, 0.0).astype(BF16)
            query_t[h] = qh.T

    own_block(range(heads // 2))

    def each(scan, *steps):
        def owner():
            order = range(CORES)
            for step in steps:
                for core in reversed(order) if scan.backward else order:
                    step(scan, core)

        pl.when(scan.owns)(owner)

    each(forward[0], Scan.sum_up)
    own_block(range(heads // 2, heads))
    wait_bytes(cot.at[:, pl.ds(0, (n_head - 1) * width)], cot_recv)
    scaled[...] = cot_block[...].astype(F32) * gain[:, cot_columns(head)]

    each(forward[0], Scan.answer, Scan.near)

    turned(range(heads))

    squares = jnp.zeros((tokens, DH), F32)
    products = jnp.zeros((tokens, DH), F32)
    for i, half in enumerate(halves):
        forward[i].receive()
        for h in half:
            prefix = forward[i].out[columns[h - half[0]], :]
            outer = dot(q[:, columns[h]], prefix, 1, 0) * scaling
            rounded = (inner[:, columns[h]] + outer).astype(BF16)
            attended[:, columns[h]] = rounded
            wide = rounded.astype(F32)
            squares = squares + wide * wide
            products = products + wide * scaled[:, columns[h]]
    square_row = jnp.sum(squares.T, axis=0, keepdims=True)
    product_row = jnp.sum(products.T, axis=0, keepdims=True)
    stat_rows = lax.broadcasted_iota(jnp.int32, stat.shape, 0)
    stat[...] = jnp.where(stat_rows == 0, square_row, product_row)

    def stat_copy(to, owner):
        return remote(
            stat, stat_in.at[owner], stat_send, stat_recv, seq, to
        )

    over_heads(lambda to: stat_copy(to, head).start())
    stat_in[head] = stat[...]
    wait_bytes(stat_in.at[pl.ds(0, n_head - 1)], stat_recv)
    summed = jnp.sum(stat_in[...], axis=0) * (1.0 / (n_head * width))
    inverse = lax.rsqrt(summed[0:1, :] + EPSILON)
    slope = inverse * inverse * inverse * summed[1:2, :]
    inverse = jnp.broadcast_to(inverse, (DH, tokens)).T
    slope = jnp.broadcast_to(slope, (DH, tokens)).T

    for i, half in enumerate(halves):
        for h in half:
            wide = attended[:, columns[h]].astype(F32)
            rounded = (inverse * scaled[:, columns[h]] - slope * wide).astype(BF16)
            grad[:, columns[h]] = rounded
            state = dot(query_t[h], rounded, 1, 0)
            backward[i].state[columns[h - half[0]], :] = state.astype(BF16)
        backward[i].send_state()

    def own_grads(h):
        at = columns[h]
        prefix = forward[h // part_heads].out[columns[h % part_heads], :]
        gh, qh, kh, vh = (ref[:, at] for ref in (grad, q, k, v))
        raw = dot(gh, vh, 1, 1) * scaling
        masked = jnp.where(rows >= cols, raw, 0.0).astype(BF16)
        raw = dot(vh, gh, 1, 1) * scaling
        masked_t = jnp.where(cols >= rows, raw, 0.0).astype(BF16)
        outer = dot(gh, prefix, 1, 1) * scaling
        gq[:, at] = (dot(masked, kh, 1, 0) + outer).astype(BF16)
        key_part[:, at] = dot(masked_t, qh, 1, 0)
        value_part[:, at] = dot(scores_t[h], gh, 1, 0)

    for h in range(heads - 2):
        own_grads(h)
    each(backward[0], Scan.sum_up)
    own_grads(heads - 2)
    each(backward[0], Scan.answer, Scan.near)
    own_grads(heads - 1)
    for i, half in enumerate(halves):
        backward[i].receive()
        for h in half:
            suffix = backward[i].out[columns[h - half[0]], :]
            outer = dot(v[:, columns[h]], suffix, 1, 1) * scaling
            gk[:, columns[h]] = (key_part[:, columns[h]] + outer).astype(BF16)
            outer = dot(k[:, columns[h]], suffix, 1, 0) * scaling
            gv[:, columns[h]] = (value_part[:, columns[h]] + outer).astype(BF16)

    for scan in scans:
        scan.drain()
    wait_bytes(cot.at[:, pl.ds(0, (n_head - 1) * width)], cot_send)
    wait_bytes(stat_in.at[pl.ds(0, n_head - 1)], stat_send)


def write_out(*refs):
    copies = [pltpu.make_async_copy(refs[i], refs[3 + i], refs[6].at[i]) for i in range(3)]
    for copy in copies:
        copy.start()
    for copy in copies:
        copy.wait()


def solution(mesh):
    n_seq, n_head = mesh.shape["seq"], mesh.shape["head"]
    size = GROUP
    groups = n_seq // size

    def local(queries, key_rows, values, cotangent, norm_gain):
        tokens, width = queries.shape
        heads = width // DH
        part = heads * DH // HALVES
        rows = part // size
        block = pltpu.VMEM((tokens, width), BF16)
        wide = pltpu.VMEM((tokens, width), F32)
        square = pltpu.VMEM((heads, DH, DH), BF16)
        scan = [
            pltpu.VMEM((part, DH), BF16),
            pltpu.VMEM((CORES, size, rows, DH), BF16),
            pltpu.VMEM((CORES, size, rows, DH), F32),
            pltpu.VMEM((CORES, rows, DH), BF16),
            pltpu.VMEM((CORES, groups - 1, rows, DH), BF16),
            pltpu.VMEM((CORES, rows, DH), F32),
            pltpu.VMEM((CORES, size, rows, DH), BF16),
            pltpu.VMEM((part, DH), BF16),
        ]
        dma = pltpu.SemaphoreType.DMA
        scan_sems = [dma, dma((CORES,))] + [dma((CORES, groups - 1))] * 2 + [dma((CORES,)), dma]
        out = pltpu.VMEM((tokens, width), BF16)
        grads = pl.pallas_call(
            functools.partial(kernel, n_seq, n_head, size),
            out_shape=(out, out, out),
            in_specs=[pl.BlockSpec(memory_space=pltpu.HBM)] * 5,
            out_specs=[pl.BlockSpec(memory_space=pltpu.VMEM)] * 3,
            scratch_shapes=[
                block,
                block,
                block,
                pltpu.VMEM(cotangent.shape, BF16),
                pltpu.VMEM((1, norm_gain.shape[0]), F32),
                block,
                wide,
                wide,
                square,
                square,
                block,
                block,
                wide,
                wide,
                pltpu.VMEM((8, tokens), F32),
                pltpu.VMEM((n_head, 8, tokens), F32),
                dma((5,)),
                dma,
                dma,
                dma,
                dma,
                *((scan + scan_sems) * (2 * HALVES)),
            ],
            compiler_params=pltpu.CompilerParams(
                collective_id=0, has_side_effects=True, vmem_limit_bytes=60 * 1024 * 1024
            ),
            cost_estimate=pl.CostEstimate(
                flops=26 * heads * DH**3, bytes_accessed=14 * tokens * width, transcendentals=0
            ),
        )(queries, key_rows, values, cotangent, norm_gain.reshape(1, -1))
        result = jax.ShapeDtypeStruct((tokens, width), BF16)
        return pl.pallas_call(
            write_out,
            out_shape=(result,) * 3,
            in_specs=[pl.BlockSpec(memory_space=pltpu.VMEM)] * 3,
            out_specs=[pl.BlockSpec(memory_space=pltpu.HBM)] * 3,
            scratch_shapes=[dma((3,))],
            compiler_params=pltpu.CompilerParams(vmem_limit_bytes=2 * 1024 * 1024),
        )(*grads)

    return jax.shard_map(
        local,
        mesh=mesh,
        in_specs=(P("seq", "head"), P("seq", "head"), P("seq", "head"), P(("seq", "head"), None), P()),
        out_specs=(P("seq", "head"), P("seq", "head"), P("seq", "head")),
        check_vma=False,
    )
```

```python
import functools

import jax
import jax.numpy as jnp
from jax import lax
from jax.experimental import pallas as pl
from jax.experimental.pallas import tpu as pltpu
from jax.sharding import PartitionSpec as P

DH = 128
EPSILON = 1e-06
GROUP = 16
HALVES = 1
CORES = 2
MESH = pl.DeviceIdType.MESH
F32 = jnp.float32
BF16 = jnp.bfloat16


def dot(left, right, left_dim, right_dim):
    dims = (((left_dim,), (right_dim,)), ((), ()))
    return lax.dot_general(left, right, dims, preferred_element_type=F32)


def remote(src, dst, send_sem, recv_sem, seq, head):
    return pltpu.make_async_remote_copy(
        src_ref=src,
        dst_ref=dst,
        send_sem=send_sem,
        recv_sem=recv_sem,
        device_id=(seq, head),
        device_id_type=MESH,
    )


def wait_bytes(ref, sem):
    pltpu.make_async_copy(ref, ref, sem).wait()


class Scan:
    def __init__(self, place, backward, state, inbox, part, total, total_in, offset, back, out, sems):
        self.seq, self.head, self.group, self.me, self.size, self.groups = place
        self.backward = backward
        self.state, self.inbox, self.part, self.total = state, inbox, part, total
        self.total_in, self.offset, self.back, self.out = total_in, offset, back, out
        self.s1, self.r1, self.s2, self.r2, self.s3, self.r3 = sems
        self.rows = inbox.shape[2]
        self.core = lax.rem(self.head, CORES)
        self.owner_head = self.head - self.core + CORES - 1
        self.owns = self.core == CORES - 1
        self.row = self.size // 4
        self.mine = self.piece(self.me, self.group)

    def slice_of(self, ref, owner):
        return ref.at[pl.ds(pl.multiple_of(owner * self.rows, self.rows), self.rows)]

    def piece(self, member, group):
        shifted = lax.rem((group + 1) // 2, 2)
        return lax.rem(member + shifted * (self.size // 2), self.size)

    def far_first(self, body, planes=slice(None)):
        here, column = self.me // self.row, lax.rem(self.me, self.row)
        rows = self.size // self.row
        others = (rows - 1 - here, lax.rem(here + 2, rows), here + 1 - 2 * lax.rem(here, 2), here)
        for other in others[planes]:
            for step in range(1, self.row + (other is not here)):
                body(other * self.row + lax.rem(column + step, self.row))

    def to_owner(self, owner):
        return remote(
            self.slice_of(self.state, self.piece(owner, self.group)),
            self.inbox.at[self.core, self.me],
            self.s1,
            self.r1.at[self.core],
            self.group * self.size + owner,
            self.owner_head,
        )

    def to_group(self, core, distance, group):
        return remote(
            self.total.at[core],
            self.total_in.at[core, distance - 1],
            self.s2.at[core, distance - 1],
            self.r2.at[core, distance - 1],
            group * self.size + self.piece(self.mine, group),
            self.head,
        )

    def to_member(self, core, member):
        return remote(
            self.back.at[core, member],
            self.slice_of(self.out, self.mine),
            self.s3.at[core],
            self.r3,
            self.group * self.size + member,
            self.head - (CORES - 1) + core,
        )

    def groups_later(self, body):
        for distance in range(1, self.groups):
            if self.backward:
                group, there = self.group - distance, self.group >= distance
            else:
                group, there = self.group + distance, self.group + distance < self.groups
            pl.when(there)(functools.partial(body, distance, group))

    def groups_earlier(self, body):
        for distance in range(1, self.groups):
            if self.backward:
                there = self.group + distance < self.groups
            else:
                there = self.group >= distance
            pl.when(there)(functools.partial(body, distance))

    def by_core(self, first, second):
        pl.when(self.core != CORES - 1)(first)
        pl.when(self.owns)(second)

    def send_state(self):
        self.far_first(lambda owner: self.to_owner(owner).start())

        def keep():
            self.inbox[CORES - 1, self.me] = self.slice_of(self.state, self.mine)[...]

        self.by_core(lambda: self.to_owner(self.me).start(), keep)

    def sum_up(self, core):
        received = self.size - (core == CORES - 1)
        wait_bytes(self.inbox.at[core, pl.ds(0, received)], self.r1.at[core])
        total = jnp.zeros(self.offset.shape[1:], F32)
        for member in range(self.size):
            total = total + self.inbox[core, member].astype(F32)
        self.total[core] = total.astype(BF16)
        self.groups_later(lambda distance, group: self.to_group(core, distance, group).start())
        self.offset[core] = jnp.zeros(self.offset.shape[1:], F32)

    def add_up(self, core):
        running = jnp.zeros(self.offset.shape[1:], F32)
        order = range(self.size)
        for member in reversed(order) if self.backward else order:
            self.part[core, member] = running
            running = running + self.inbox[core, member].astype(F32)

    def in_order(self, body):
        here, column = self.me // self.row, lax.rem(self.me, self.row)
        for other in range(self.size // self.row):
            pl.when(here != other)(functools.partial(body, other * self.row + column))
            for step in range(1, self.row):
                body(other * self.row + lax.rem(column + step, self.row))

    def near(self, core):
        if not self.backward:
            self.far_first(lambda member: self.to_member(core, member).start(), slice(2, 4))
        if core == CORES - 1:
            self.slice_of(self.out, self.mine)[...] = self.back[core, self.me]
        else:
            self.to_member(core, self.me).start()

    def answer(self, core):
        def add(distance):
            self.to_group(core, distance, self.group).wait_recv()
            self.offset[core] += self.total_in[core, distance - 1].astype(F32)

        self.groups_earlier(add)
        self.back[core] = (self.offset[core][None] + self.part[core]).astype(BF16)
        if self.backward:
            self.in_order(lambda member: self.to_member(core, member).start())
        else:
            self.far_first(lambda member: self.to_member(core, member).start(), slice(0, 2))

    def receive(self):
        def wait(count):
            wait_bytes(self.back.at[0, pl.ds(0, count)], self.r3)

        self.by_core(lambda: wait(self.size), lambda: wait(self.size - 1))

    def drain(self):
        def sent(count):
            wait_bytes(self.inbox.at[0, pl.ds(0, count)], self.s1)

        def owner_sent():
            sent(self.size - 1)
            for core in range(CORES):
                self.groups_later(lambda distance, group: self.to_group(core, distance, group).wait_send())
                wait_bytes(self.back.at[core, pl.ds(0, self.size - (core == CORES - 1))], self.s3.at[core])

        self.by_core(lambda: sent(self.size), owner_sent)


def kernel(n_seq, n_head, size, *refs):
    q_hbm, k_hbm, v_hbm, cot_hbm, gain_hbm, gq, gk, gv = refs[:8]
    q, k, v, cot, gain, cot_block, scaled, inner, scores_t, query_t = refs[8:18]
    attended, grad, key_part, value_part, stat, stat_in = refs[18:24]
    local_sems, cot_send, cot_recv, stat_send, stat_recv = refs[24:29]
    scan_refs = [refs[at : at + 14] for at in range(29, 29 + 14 * 2 * HALVES, 14)]

    seq, head = lax.axis_index("seq"), lax.axis_index("head")
    groups = n_seq // size
    group, me = seq // size, lax.rem(seq, size)
    tokens, width = q.shape
    heads = width // DH
    cot_rows = cot.shape[0]
    scaling = DH ** (-0.5)
    place = (seq, head, group, me, size, groups)
    scans = [Scan(place, i >= HALVES, *own[:8], own[8:]) for i, own in enumerate(scan_refs)]
    forward, backward = scans[:HALVES], scans[HALVES:]
    columns = [slice(h * DH, (h + 1) * DH) for h in range(heads)]
    part_heads = heads // HALVES
    halves = [range(i * part_heads, (i + 1) * part_heads) for i in range(HALVES)]

    loads = [
        pltpu.make_async_copy(src, dst, local_sems.at[i])
        for i, (src, dst) in enumerate(
            [(k_hbm, k), (v_hbm, v), (cot_hbm, cot), (q_hbm, q), (gain_hbm, gain)]
        )
    ]
    for load in loads[:2]:
        load.start()

    barrier = pltpu.get_barrier_semaphore()

    def greet(other_seq, other_head):
        pl.semaphore_signal(
            barrier, inc=1, device_id=(other_seq, other_head), device_id_type=MESH
        )

    def greet_owners():
        forward[0].far_first(lambda member: greet(group * size + member, head + 1))

    def greet_owned():
        for step in range(1, groups):
            other = lax.rem(group + step, groups)
            greet(other * size + forward[0].piece(forward[0].mine, other), head)
        forward[0].far_first(lambda member: greet(group * size + member, head - 1))
        forward[0].far_first(lambda member: greet(group * size + member, head))

    forward[0].by_core(greet_owners, greet_owned)
    for step in range(1, n_head):
        greet(seq, lax.rem(head + step, n_head))
    for load in loads[2:]:
        load.start()

    loads[0].wait()
    loads[1].wait()
    for i, half in enumerate(halves):
        for h in half:
            state = dot(k[:, columns[h]], v[:, columns[h]], 0, 0)
            forward[i].state[columns[h - half[0]], :] = state.astype(BF16)
        if i == 0:
            forward[0].by_core(
                lambda: pl.semaphore_wait(barrier, size - 1 + n_head - 1),
                lambda: pl.semaphore_wait(barrier, 2 * (size - 1) + groups - 1 + n_head - 1),
            )
        forward[i].send_state()

    def cot_columns(to):
        return pl.ds(pl.multiple_of(to * width, width), width)

    def cot_rows_of(owner):
        return cot_block.at[pl.ds(pl.multiple_of(owner * cot_rows, cot_rows), cot_rows)]

    def cot_copy(to, owner):
        return remote(
            cot.at[:, cot_columns(to)],
            cot_rows_of(owner),
            cot_send,
            cot_recv,
            seq,
            to,
        )

    def over_heads(body):
        for step in range(1, n_head):
            body(lax.rem(head + step, n_head))

    loads[2].wait()
    over_heads(lambda to: cot_copy(to, head).start())
    cot_rows_of(head)[...] = cot[:, cot_columns(head)]

    loads[3].wait()
    loads[4].wait()
    rows = lax.broadcasted_iota(jnp.int32, (tokens, tokens), 0)
    cols = lax.broadcasted_iota(jnp.int32, (tokens, tokens), 1)

    def own_block(some):
        for h in some:
            qh, kh, vh = (ref[:, columns[h]] for ref in (q, k, v))
            raw = dot(qh, kh, 1, 1) * scaling
            masked = jnp.where(rows >= cols, raw, 0.0).astype(BF16)
            inner[:, columns[h]] = dot(masked, vh, 1, 0)

    def turned(some):
        for h in some:
            qh, kh = q[:, columns[h]], k[:, columns[h]]
            raw = dot(kh, qh, 1, 1) * scaling
            scores_t[h] = jnp.where(cols >= rows, raw, 0.0).astype(BF16)
            query_t[h] = qh.T

    own_block(range(heads // 2))

    def each(scan, *steps):
        def owner():
            order = range(CORES)
            for step in steps:
                for core in reversed(order) if scan.backward else order:
                    step(scan, core)

        pl.when(scan.owns)(owner)

    each(forward[0], Scan.sum_up, Scan.add_up)
    own_block(range(heads // 2, heads))
    wait_bytes(cot.at[:, pl.ds(0, (n_head - 1) * width)], cot_recv)
    scaled[...] = cot_block[...].astype(F32) * gain[:, cot_columns(head)]

    each(forward[0], Scan.answer, Scan.near)

    turned(range(heads))

    squares = jnp.zeros((tokens, DH), F32)
    products = jnp.zeros((tokens, DH), F32)
    for i, half in enumerate(halves):
        forward[i].receive()
        for h in half:
            prefix = forward[i].out[columns[h - half[0]], :]
            outer = dot(q[:, columns[h]], prefix, 1, 0) * scaling
            rounded = (inner[:, columns[h]] + outer).astype(BF16)
            attended[:, columns[h]] = rounded
            wide = rounded.astype(F32)
            squares = squares + wide * wide
            products = products + wide * scaled[:, columns[h]]
    square_row = jnp.sum(squares.T, axis=0, keepdims=True)
    product_row = jnp.sum(products.T, axis=0, keepdims=True)
    stat_rows = lax.broadcasted_iota(jnp.int32, stat.shape, 0)
    stat[...] = jnp.where(stat_rows == 0, square_row, product_row)

    def stat_copy(to, owner):
        return remote(
            stat, stat_in.at[owner], stat_send, stat_recv, seq, to
        )

    over_heads(lambda to: stat_copy(to, head).start())
    stat_in[head] = stat[...]
    wait_bytes(stat_in.at[pl.ds(0, n_head - 1)], stat_recv)
    summed = jnp.sum(stat_in[...], axis=0) * (1.0 / (n_head * width))
    inverse = lax.rsqrt(summed[0:1, :] + EPSILON)
    slope = inverse * inverse * inverse * summed[1:2, :]
    inverse = jnp.broadcast_to(inverse, (DH, tokens)).T
    slope = jnp.broadcast_to(slope, (DH, tokens)).T

    for i, half in enumerate(halves):
        for h in half:
            wide = attended[:, columns[h]].astype(F32)
            rounded = (inverse * scaled[:, columns[h]] - slope * wide).astype(BF16)
            grad[:, columns[h]] = rounded
            state = dot(query_t[h], rounded, 1, 0)
            backward[i].state[columns[h - half[0]], :] = state.astype(BF16)
        backward[i].send_state()

    def own_grads(h):
        at = columns[h]
        prefix = forward[h // part_heads].out[columns[h % part_heads], :]
        gh, qh, kh, vh = (ref[:, at] for ref in (grad, q, k, v))
        raw = dot(gh, vh, 1, 1) * scaling
        masked = jnp.where(rows >= cols, raw, 0.0).astype(BF16)
        raw = dot(vh, gh, 1, 1) * scaling
        masked_t = jnp.where(cols >= rows, raw, 0.0).astype(BF16)
        outer = dot(gh, prefix, 1, 1) * scaling
        gq[:, at] = (dot(masked, kh, 1, 0) + outer).astype(BF16)
        key_part[:, at] = dot(masked_t, qh, 1, 0)
        value_part[:, at] = dot(scores_t[h], gh, 1, 0)

    for h in range(heads - 2):
        own_grads(h)
    each(backward[0], Scan.sum_up, Scan.add_up)
    own_grads(heads - 2)
    each(backward[0], Scan.answer, Scan.near)
    own_grads(heads - 1)
    for i, half in enumerate(halves):
        backward[i].receive()
        for h in half:
            suffix = backward[i].out[columns[h - half[0]], :]
            outer = dot(v[:, columns[h]], suffix, 1, 1) * scaling
            gk[:, columns[h]] = (key_part[:, columns[h]] + outer).astype(BF16)
            outer = dot(k[:, columns[h]], suffix, 1, 0) * scaling
            gv[:, columns[h]] = (value_part[:, columns[h]] + outer).astype(BF16)

    for scan in scans:
        scan.drain()
    wait_bytes(cot.at[:, pl.ds(0, (n_head - 1) * width)], cot_send)
    wait_bytes(stat_in.at[pl.ds(0, n_head - 1)], stat_send)


def write_out(*refs):
    copies = [pltpu.make_async_copy(refs[i], refs[3 + i], refs[6].at[i]) for i in range(3)]
    for copy in copies:
        copy.start()
    for copy in copies:
        copy.wait()


def solution(mesh):
    n_seq, n_head = mesh.shape["seq"], mesh.shape["head"]
    size = GROUP
    groups = n_seq // size

    def local(queries, key_rows, values, cotangent, norm_gain):
        tokens, width = queries.shape
        heads = width // DH
        part = heads * DH // HALVES
        rows = part // size
        block = pltpu.VMEM((tokens, width), BF16)
        wide = pltpu.VMEM((tokens, width), F32)
        square = pltpu.VMEM((heads, DH, DH), BF16)
        scan = [
            pltpu.VMEM((part, DH), BF16),
            pltpu.VMEM((CORES, size, rows, DH), BF16),
            pltpu.VMEM((CORES, size, rows, DH), F32),
            pltpu.VMEM((CORES, rows, DH), BF16),
            pltpu.VMEM((CORES, groups - 1, rows, DH), BF16),
            pltpu.VMEM((CORES, rows, DH), F32),
            pltpu.VMEM((CORES, size, rows, DH), BF16),
            pltpu.VMEM((part, DH), BF16),
        ]
        dma = pltpu.SemaphoreType.DMA
        scan_sems = [dma, dma((CORES,))] + [dma((CORES, groups - 1))] * 2 + [dma((CORES,)), dma]
        out = pltpu.VMEM((tokens, width), BF16)
        grads = pl.pallas_call(
            functools.partial(kernel, n_seq, n_head, size),
            out_shape=(out, out, out),
            in_specs=[pl.BlockSpec(memory_space=pltpu.HBM)] * 5,
            out_specs=[pl.BlockSpec(memory_space=pltpu.VMEM)] * 3,
            scratch_shapes=[
                block,
                block,
                block,
                pltpu.VMEM(cotangent.shape, BF16),
                pltpu.VMEM((1, norm_gain.shape[0]), F32),
                block,
                wide,
                wide,
                square,
                square,
                block,
                block,
                wide,
                wide,
                pltpu.VMEM((8, tokens), F32),
                pltpu.VMEM((n_head, 8, tokens), F32),
                dma((5,)),
                dma,
                dma,
                dma,
                dma,
                *((scan + scan_sems) * (2 * HALVES)),
            ],
            compiler_params=pltpu.CompilerParams(
                collective_id=0, has_side_effects=True, vmem_limit_bytes=60 * 1024 * 1024
            ),
            cost_estimate=pl.CostEstimate(
                flops=26 * heads * DH**3, bytes_accessed=14 * tokens * width, transcendentals=0
            ),
        )(queries, key_rows, values, cotangent, norm_gain.reshape(1, -1))
        result = jax.ShapeDtypeStruct((tokens, width), BF16)
        return pl.pallas_call(
            write_out,
            out_shape=(result,) * 3,
            in_specs=[pl.BlockSpec(memory_space=pltpu.VMEM)] * 3,
            out_specs=[pl.BlockSpec(memory_space=pltpu.HBM)] * 3,
            scratch_shapes=[dma((3,))],
            compiler_params=pltpu.CompilerParams(vmem_limit_bytes=2 * 1024 * 1024),
        )(*grads)

    return jax.shard_map(
        local,
        mesh=mesh,
        in_specs=(P("seq", "head"), P("seq", "head"), P("seq", "head"), P(("seq", "head"), None), P()),
        out_specs=(P("seq", "head"), P("seq", "head"), P("seq", "head")),
        check_vma=False,
    )
```

```python
import functools

import jax
import jax.numpy as jnp
from jax import lax
from jax.experimental import pallas as pl
from jax.experimental.pallas import tpu as pltpu
from jax.sharding import PartitionSpec as P

DH = 128
EPSILON = 1e-06
GROUP = 16
HALVES = 1
CORES = 2
MESH = pl.DeviceIdType.MESH
F32 = jnp.float32
BF16 = jnp.bfloat16


def dot(left, right, left_dim, right_dim):
    dims = (((left_dim,), (right_dim,)), ((), ()))
    return lax.dot_general(left, right, dims, preferred_element_type=F32)


def remote(src, dst, send_sem, recv_sem, seq, head):
    return pltpu.make_async_remote_copy(
        src_ref=src,
        dst_ref=dst,
        send_sem=send_sem,
        recv_sem=recv_sem,
        device_id=(seq, head),
        device_id_type=MESH,
    )


def wait_bytes(ref, sem):
    pltpu.make_async_copy(ref, ref, sem).wait()


class Scan:
    def __init__(self, place, backward, state, inbox, part, total, total_in, offset, back, out, sems):
        self.seq, self.head, self.group, self.me, self.size, self.groups = place
        self.backward = backward
        self.state, self.inbox, self.part, self.total = state, inbox, part, total
        self.total_in, self.offset, self.back, self.out = total_in, offset, back, out
        self.s1, self.r1, self.s2, self.r2, self.s3, self.r3 = sems
        self.rows = inbox.shape[2]
        self.core = lax.rem(self.head, CORES)
        self.owner_head = self.head - self.core + CORES - 1
        self.owns = self.core == CORES - 1
        self.row = self.size // 4
        self.mine = self.piece(self.me, self.group)

    def slice_of(self, ref, owner):
        return ref.at[pl.ds(pl.multiple_of(owner * self.rows, self.rows), self.rows)]

    def piece(self, member, group):
        shifted = lax.rem((group + 1) // 2, 2)
        return lax.rem(member + shifted * (self.size // 2), self.size)

    def far_first(self, *bodies, planes=slice(None)):
        here, column = self.me // self.row, lax.rem(self.me, self.row)
        rows = self.size // self.row
        others = (rows - 1 - here, lax.rem(here + 2, rows), here + 1 - 2 * lax.rem(here, 2), here)
        for other in others[planes]:
            for step in range(1, self.row + (other is not here)):
                for body in bodies:
                    body(other * self.row + lax.rem(column + step, self.row))

    def to_owner(self, owner):
        return remote(
            self.slice_of(self.state, self.piece(owner, self.group)),
            self.inbox.at[self.core, self.me],
            self.s1,
            self.r1.at[self.core],
            self.group * self.size + owner,
            self.owner_head,
        )

    def to_group(self, core, distance, group):
        return remote(
            self.total.at[core],
            self.total_in.at[core, distance - 1],
            self.s2.at[core, distance - 1],
            self.r2.at[core, distance - 1],
            group * self.size + self.piece(self.mine, group),
            self.head,
        )

    def to_member(self, core, member):
        return remote(
            self.back.at[core, member],
            self.slice_of(self.out, self.mine),
            self.s3.at[core],
            self.r3,
            self.group * self.size + member,
            self.head - (CORES - 1) + core,
        )

    def groups_later(self, body):
        for distance in range(1, self.groups):
            if self.backward:
                group, there = self.group - distance, self.group >= distance
            else:
                group, there = self.group + distance, self.group + distance < self.groups
            pl.when(there)(functools.partial(body, distance, group))

    def groups_earlier(self, body):
        for distance in range(1, self.groups):
            if self.backward:
                there = self.group + distance < self.groups
            else:
                there = self.group >= distance
            pl.when(there)(functools.partial(body, distance))

    def by_core(self, first, second):
        pl.when(self.core != CORES - 1)(first)
        pl.when(self.owns)(second)

    def send_state(self):
        self.far_first(lambda owner: self.to_owner(owner).start())

        def keep():
            self.inbox[CORES - 1, self.me] = self.slice_of(self.state, self.mine)[...]

        self.by_core(lambda: self.to_owner(self.me).start(), keep)

    def sum_up(self, core):
        received = self.size - (core == CORES - 1)
        wait_bytes(self.inbox.at[core, pl.ds(0, received)], self.r1.at[core])
        total = jnp.zeros(self.offset.shape[1:], F32)
        for member in range(self.size):
            total = total + self.inbox[core, member].astype(F32)
        self.total[core] = total.astype(BF16)
        self.groups_later(lambda distance, group: self.to_group(core, distance, group).start())
        self.offset[core] = jnp.zeros(self.offset.shape[1:], F32)

    def add_up(self, core):
        running = jnp.zeros(self.offset.shape[1:], F32)
        order = range(self.size)
        for member in reversed(order) if self.backward else order:
            self.part[core, member] = running
            running = running + self.inbox[core, member].astype(F32)

    def in_order(self, body):
        here, column = self.me // self.row, lax.rem(self.me, self.row)
        for other in range(self.size // self.row):
            pl.when(here != other)(functools.partial(body, other * self.row + column))
            for step in range(1, self.row):
                body(other * self.row + lax.rem(column + step, self.row))

    def near(self, core):
        if not self.backward:
            self.far_first(lambda member: self.to_member(core, member).start(), planes=slice(2, 4))
        if core == CORES - 1:
            self.slice_of(self.out, self.mine)[...] = self.back[core, self.me]
        else:
            self.to_member(core, self.me).start()

    def answer(self, core):
        def add(distance):
            self.to_group(core, distance, self.group).wait_recv()
            self.offset[core] += self.total_in[core, distance - 1].astype(F32)

        self.groups_earlier(add)
        self.back[core] = (self.offset[core][None] + self.part[core]).astype(BF16)
        if self.backward:
            self.in_order(lambda member: self.to_member(core, member).start())
        else:
            self.far_first(lambda member: self.to_member(core, member).start(), planes=slice(0, 2))

    def receive(self):
        def wait(count):
            wait_bytes(self.back.at[0, pl.ds(0, count)], self.r3)

        self.by_core(lambda: wait(self.size), lambda: wait(self.size - 1))

    def drain(self):
        def sent(count):
            wait_bytes(self.inbox.at[0, pl.ds(0, count)], self.s1)

        def owner_sent():
            sent(self.size - 1)
            for core in range(CORES):
                self.groups_later(lambda distance, group: self.to_group(core, distance, group).wait_send())
                wait_bytes(self.back.at[core, pl.ds(0, self.size - (core == CORES - 1))], self.s3.at[core])

        self.by_core(lambda: sent(self.size), owner_sent)


def kernel(n_seq, n_head, size, *refs):
    q_hbm, k_hbm, v_hbm, cot_hbm, gain_hbm, gq, gk, gv = refs[:8]
    q, k, v, cot, gain, cot_block, scaled, inner, scores_t, query_t = refs[8:18]
    attended, grad, key_part, value_part, stat, stat_in = refs[18:24]
    local_sems, cot_send, cot_recv, stat_send, stat_recv = refs[24:29]
    scan_refs = [refs[at : at + 14] for at in range(29, 29 + 14 * 2 * HALVES, 14)]

    seq, head = lax.axis_index("seq"), lax.axis_index("head")
    groups = n_seq // size
    group, me = seq // size, lax.rem(seq, size)
    tokens, width = q.shape
    heads = width // DH
    cot_rows = cot.shape[0]
    scaling = DH ** (-0.5)
    place = (seq, head, group, me, size, groups)
    scans = [Scan(place, i >= HALVES, *own[:8], own[8:]) for i, own in enumerate(scan_refs)]
    forward, backward = scans[:HALVES], scans[HALVES:]
    columns = [slice(h * DH, (h + 1) * DH) for h in range(heads)]
    part_heads = heads // HALVES
    halves = [range(i * part_heads, (i + 1) * part_heads) for i in range(HALVES)]

    loads = [
        pltpu.make_async_copy(src, dst, local_sems.at[i])
        for i, (src, dst) in enumerate(
            [(k_hbm, k), (v_hbm, v), (cot_hbm, cot), (q_hbm, q), (gain_hbm, gain)]
        )
    ]
    for load in loads[:2]:
        load.start()

    barrier = pltpu.get_barrier_semaphore()

    def greet(other_seq, other_head):
        pl.semaphore_signal(
            barrier, inc=1, device_id=(other_seq, other_head), device_id_type=MESH
        )

    def greet_owners():
        forward[0].far_first(lambda member: greet(group * size + member, head + 1))

    def greet_owned():
        for step in range(1, groups):
            other = lax.rem(group + step, groups)
            greet(other * size + forward[0].piece(forward[0].mine, other), head)
        forward[0].far_first(
            lambda member: greet(group * size + member, head),
            lambda member: greet(group * size + member, head - 1),
        )

    forward[0].by_core(greet_owners, greet_owned)
    for step in range(1, n_head):
        greet(seq, lax.rem(head + step, n_head))
    for load in loads[2:]:
        load.start()

    loads[0].wait()
    loads[1].wait()
    for i, half in enumerate(halves):
        for h in half:
            state = dot(k[:, columns[h]], v[:, columns[h]], 0, 0)
            forward[i].state[columns[h - half[0]], :] = state.astype(BF16)
        if i == 0:
            forward[0].by_core(
                lambda: pl.semaphore_wait(barrier, size - 1 + n_head - 1),
                lambda: pl.semaphore_wait(barrier, 2 * (size - 1) + groups - 1 + n_head - 1),
            )
        forward[i].send_state()

    def cot_columns(to):
        return pl.ds(pl.multiple_of(to * width, width), width)

    def cot_rows_of(owner):
        return cot_block.at[pl.ds(pl.multiple_of(owner * cot_rows, cot_rows), cot_rows)]

    def cot_copy(to, owner):
        return remote(
            cot.at[:, cot_columns(to)],
            cot_rows_of(owner),
            cot_send,
            cot_recv,
            seq,
            to,
        )

    def over_heads(body):
        for step in range(1, n_head):
            body(lax.rem(head + step, n_head))

    loads[2].wait()
    over_heads(lambda to: cot_copy(to, head).start())
    cot_rows_of(head)[...] = cot[:, cot_columns(head)]

    loads[3].wait()
    loads[4].wait()
    rows = lax.broadcasted_iota(jnp.int32, (tokens, tokens), 0)
    cols = lax.broadcasted_iota(jnp.int32, (tokens, tokens), 1)

    def own_block(some):
        for h in some:
            qh, kh, vh = (ref[:, columns[h]] for ref in (q, k, v))
            raw = dot(qh, kh, 1, 1) * scaling
            masked = jnp.where(rows >= cols, raw, 0.0).astype(BF16)
            inner[:, columns[h]] = dot(masked, vh, 1, 0)

    def turned(some):
        for h in some:
            qh, kh = q[:, columns[h]], k[:, columns[h]]
            raw = dot(kh, qh, 1, 1) * scaling
            scores_t[h] = jnp.where(cols >= rows, raw, 0.0).astype(BF16)
            query_t[h] = qh.T

    own_block(range(heads // 2))

    def each(scan, *steps):
        def owner():
            order = range(CORES)
            for step in steps:
                for core in reversed(order) if scan.backward else order:
                    step(scan, core)

        pl.when(scan.owns)(owner)

    each(forward[0], Scan.sum_up, Scan.add_up)
    own_block(range(heads // 2, heads))
    wait_bytes(cot.at[:, pl.ds(0, (n_head - 1) * width)], cot_recv)
    scaled[...] = cot_block[...].astype(F32) * gain[:, cot_columns(head)]

    each(forward[0], Scan.answer, Scan.near)

    turned(range(heads))

    squares = jnp.zeros((tokens, DH), F32)
    products = jnp.zeros((tokens, DH), F32)
    for i, half in enumerate(halves):
        forward[i].receive()
        for h in half:
            prefix = forward[i].out[columns[h - half[0]], :]
            outer = dot(q[:, columns[h]], prefix, 1, 0) * scaling
            rounded = (inner[:, columns[h]] + outer).astype(BF16)
            attended[:, columns[h]] = rounded
            wide = rounded.astype(F32)
            squares = squares + wide * wide
            products = products + wide * scaled[:, columns[h]]
    square_row = jnp.sum(squares.T, axis=0, keepdims=True)
    product_row = jnp.sum(products.T, axis=0, keepdims=True)
    stat_rows = lax.broadcasted_iota(jnp.int32, stat.shape, 0)
    stat[...] = jnp.where(stat_rows == 0, square_row, product_row)

    def stat_copy(to, owner):
        return remote(
            stat, stat_in.at[owner], stat_send, stat_recv, seq, to
        )

    over_heads(lambda to: stat_copy(to, head).start())
    stat_in[head] = stat[...]
    wait_bytes(stat_in.at[pl.ds(0, n_head - 1)], stat_recv)
    summed = jnp.sum(stat_in[...], axis=0) * (1.0 / (n_head * width))
    inverse = lax.rsqrt(summed[0:1, :] + EPSILON)
    slope = inverse * inverse * inverse * summed[1:2, :]
    inverse = jnp.broadcast_to(inverse, (DH, tokens)).T
    slope = jnp.broadcast_to(slope, (DH, tokens)).T

    for i, half in enumerate(halves):
        for h in half:
            wide = attended[:, columns[h]].astype(F32)
            rounded = (inverse * scaled[:, columns[h]] - slope * wide).astype(BF16)
            grad[:, columns[h]] = rounded
            state = dot(query_t[h], rounded, 1, 0)
            backward[i].state[columns[h - half[0]], :] = state.astype(BF16)
        backward[i].send_state()

    def own_grads(h):
        at = columns[h]
        prefix = forward[h // part_heads].out[columns[h % part_heads], :]
        gh, qh, kh, vh = (ref[:, at] for ref in (grad, q, k, v))
        raw = dot(gh, vh, 1, 1) * scaling
        masked = jnp.where(rows >= cols, raw, 0.0).astype(BF16)
        raw = dot(vh, gh, 1, 1) * scaling
        masked_t = jnp.where(cols >= rows, raw, 0.0).astype(BF16)
        outer = dot(gh, prefix, 1, 1) * scaling
        gq[:, at] = (dot(masked, kh, 1, 0) + outer).astype(BF16)
        key_part[:, at] = dot(masked_t, qh, 1, 0)
        value_part[:, at] = dot(scores_t[h], gh, 1, 0)

    for h in range(heads - 2):
        own_grads(h)
    each(backward[0], Scan.sum_up, Scan.add_up)
    own_grads(heads - 2)
    each(backward[0], Scan.answer, Scan.near)
    own_grads(heads - 1)
    for i, half in enumerate(halves):
        backward[i].receive()
        for h in half:
            suffix = backward[i].out[columns[h - half[0]], :]
            outer = dot(v[:, columns[h]], suffix, 1, 1) * scaling
            gk[:, columns[h]] = (key_part[:, columns[h]] + outer).astype(BF16)
            outer = dot(k[:, columns[h]], suffix, 1, 0) * scaling
            gv[:, columns[h]] = (value_part[:, columns[h]] + outer).astype(BF16)

    for scan in scans:
        scan.drain()
    wait_bytes(cot.at[:, pl.ds(0, (n_head - 1) * width)], cot_send)
    wait_bytes(stat_in.at[pl.ds(0, n_head - 1)], stat_send)


def write_out(*refs):
    copies = [pltpu.make_async_copy(refs[i], refs[3 + i], refs[6].at[i]) for i in range(3)]
    for copy in copies:
        copy.start()
    for copy in copies:
        copy.wait()


def solution(mesh):
    n_seq, n_head = mesh.shape["seq"], mesh.shape["head"]
    size = GROUP
    groups = n_seq // size

    def local(queries, key_rows, values, cotangent, norm_gain):
        tokens, width = queries.shape
        heads = width // DH
        part = heads * DH // HALVES
        rows = part // size
        block = pltpu.VMEM((tokens, width), BF16)
        wide = pltpu.VMEM((tokens, width), F32)
        square = pltpu.VMEM((heads, DH, DH), BF16)
        scan = [
            pltpu.VMEM((part, DH), BF16),
            pltpu.VMEM((CORES, size, rows, DH), BF16),
            pltpu.VMEM((CORES, size, rows, DH), F32),
            pltpu.VMEM((CORES, rows, DH), BF16),
            pltpu.VMEM((CORES, groups - 1, rows, DH), BF16),
            pltpu.VMEM((CORES, rows, DH), F32),
            pltpu.VMEM((CORES, size, rows, DH), BF16),
            pltpu.VMEM((part, DH), BF16),
        ]
        dma = pltpu.SemaphoreType.DMA
        scan_sems = [dma, dma((CORES,))] + [dma((CORES, groups - 1))] * 2 + [dma((CORES,)), dma]
        out = pltpu.VMEM((tokens, width), BF16)
        grads = pl.pallas_call(
            functools.partial(kernel, n_seq, n_head, size),
            out_shape=(out, out, out),
            in_specs=[pl.BlockSpec(memory_space=pltpu.HBM)] * 5,
            out_specs=[pl.BlockSpec(memory_space=pltpu.VMEM)] * 3,
            scratch_shapes=[
                block,
                block,
                block,
                pltpu.VMEM(cotangent.shape, BF16),
                pltpu.VMEM((1, norm_gain.shape[0]), F32),
                block,
                wide,
                wide,
                square,
                square,
                block,
                block,
                wide,
                wide,
                pltpu.VMEM((8, tokens), F32),
                pltpu.VMEM((n_head, 8, tokens), F32),
                dma((5,)),
                dma,
                dma,
                dma,
                dma,
                *((scan + scan_sems) * (2 * HALVES)),
            ],
            compiler_params=pltpu.CompilerParams(
                collective_id=0, has_side_effects=True, vmem_limit_bytes=60 * 1024 * 1024
            ),
            cost_estimate=pl.CostEstimate(
                flops=26 * heads * DH**3, bytes_accessed=14 * tokens * width, transcendentals=0
            ),
        )(queries, key_rows, values, cotangent, norm_gain.reshape(1, -1))
        result = jax.ShapeDtypeStruct((tokens, width), BF16)
        return pl.pallas_call(
            write_out,
            out_shape=(result,) * 3,
            in_specs=[pl.BlockSpec(memory_space=pltpu.VMEM)] * 3,
            out_specs=[pl.BlockSpec(memory_space=pltpu.HBM)] * 3,
            scratch_shapes=[dma((3,))],
            compiler_params=pltpu.CompilerParams(vmem_limit_bytes=2 * 1024 * 1024),
        )(*grads)

    return jax.shard_map(
        local,
        mesh=mesh,
        in_specs=(P("seq", "head"), P("seq", "head"), P("seq", "head"), P(("seq", "head"), None), P()),
        out_specs=(P("seq", "head"), P("seq", "head"), P("seq", "head")),
        check_vma=False,
    )
```

```python
import functools

import jax
import jax.numpy as jnp
from jax import lax
from jax.experimental import pallas as pl
from jax.experimental.pallas import tpu as pltpu
from jax.sharding import PartitionSpec as P

DH = 128
EPSILON = 1e-06
GROUP = 16
HALVES = 1
CORES = 2
MESH = pl.DeviceIdType.MESH
F32 = jnp.float32
BF16 = jnp.bfloat16


def dot(left, right, left_dim, right_dim):
    dims = (((left_dim,), (right_dim,)), ((), ()))
    return lax.dot_general(left, right, dims, preferred_element_type=F32)


def remote(src, dst, send_sem, recv_sem, seq, head):
    return pltpu.make_async_remote_copy(
        src_ref=src,
        dst_ref=dst,
        send_sem=send_sem,
        recv_sem=recv_sem,
        device_id=(seq, head),
        device_id_type=MESH,
    )


def wait_bytes(ref, sem):
    pltpu.make_async_copy(ref, ref, sem).wait()


class Scan:
    def __init__(self, place, backward, state, inbox, part, total, total_in, offset, back, out, sems):
        self.seq, self.head, self.group, self.me, self.size, self.groups = place
        self.backward = backward
        self.state, self.inbox, self.part, self.total = state, inbox, part, total
        self.total_in, self.offset, self.back, self.out = total_in, offset, back, out
        self.s1, self.r1, self.s2, self.r2, self.s3, self.r3 = sems
        self.rows = inbox.shape[2]
        self.core = lax.rem(self.head, CORES)
        self.owner_head = self.head - self.core + CORES - 1
        self.owns = self.core == CORES - 1
        self.row = self.size // 4
        self.mine = self.piece(self.me, self.group)

    def slice_of(self, ref, owner):
        return ref.at[pl.ds(pl.multiple_of(owner * self.rows, self.rows), self.rows)]

    def piece(self, member, group):
        shifted = lax.rem((group + 1) // 2, 2)
        return lax.rem(member + shifted * (self.size // 2), self.size)

    def far_first(self, *bodies, planes=slice(None)):
        here, column = self.me // self.row, lax.rem(self.me, self.row)
        rows = self.size // self.row
        others = (rows - 1 - here, lax.rem(here + 2, rows), here + 1 - 2 * lax.rem(here, 2), here)
        for other in others[planes]:
            for step in range(1, self.row + (other is not here)):
                for body in bodies:
                    body(other * self.row + lax.rem(column + step, self.row))

    def to_owner(self, owner):
        return remote(
            self.slice_of(self.state, self.piece(owner, self.group)),
            self.inbox.at[self.core, self.me],
            self.s1,
            self.r1.at[self.core],
            self.group * self.size + owner,
            self.owner_head,
        )

    def to_group(self, core, distance, group):
        return remote(
            self.total.at[core],
            self.total_in.at[core, distance - 1],
            self.s2.at[core, distance - 1],
            self.r2.at[core, distance - 1],
            group * self.size + self.piece(self.mine, group),
            self.head,
        )

    def to_member(self, core, member):
        return remote(
            self.back.at[core, member],
            self.slice_of(self.out, self.mine),
            self.s3.at[core],
            self.r3,
            self.group * self.size + member,
            self.head - (CORES - 1) + core,
        )

    def groups_later(self, body):
        for distance in range(1, self.groups):
            if self.backward:
                group, there = self.group - distance, self.group >= distance
            else:
                group, there = self.group + distance, self.group + distance < self.groups
            pl.when(there)(functools.partial(body, distance, group))

    def groups_earlier(self, body):
        for distance in range(1, self.groups):
            if self.backward:
                there = self.group + distance < self.groups
            else:
                there = self.group >= distance
            pl.when(there)(functools.partial(body, distance))

    def by_core(self, first, second):
        pl.when(self.core != CORES - 1)(first)
        pl.when(self.owns)(second)

    def send_state(self):
        far, near = slice(None), slice(None, None, -1)

        def send(planes):
            self.far_first(lambda owner: self.to_owner(owner).start(), planes=planes)

        def first():
            send(near if self.backward else far)
            self.to_owner(self.me).start()

        def second():
            send(far if self.backward else near)
            self.inbox[CORES - 1, self.me] = self.slice_of(self.state, self.mine)[...]

        self.by_core(first, second)

    def sum_up(self, core):
        received = self.size - (core == CORES - 1)
        wait_bytes(self.inbox.at[core, pl.ds(0, received)], self.r1.at[core])
        total = jnp.zeros(self.offset.shape[1:], F32)
        for member in range(self.size):
            total = total + self.inbox[core, member].astype(F32)
        self.total[core] = total.astype(BF16)
        self.groups_later(lambda distance, group: self.to_group(core, distance, group).start())
        self.offset[core] = jnp.zeros(self.offset.shape[1:], F32)

    def add_up(self, core):
        running = jnp.zeros(self.offset.shape[1:], F32)
        order = range(self.size)
        for member in reversed(order) if self.backward else order:
            self.part[core, member] = running
            running = running + self.inbox[core, member].astype(F32)

    def in_order(self, body):
        here, column = self.me // self.row, lax.rem(self.me, self.row)
        for other in range(self.size // self.row):
            pl.when(here != other)(functools.partial(body, other * self.row + column))
            for step in range(1, self.row):
                body(other * self.row + lax.rem(column + step, self.row))

    def near(self, core):
        if not self.backward:
            self.far_first(lambda member: self.to_member(core, member).start(), planes=slice(2, 4))
        if core == CORES - 1:
            self.slice_of(self.out, self.mine)[...] = self.back[core, self.me]
        else:
            self.to_member(core, self.me).start()

    def answer(self, core):
        def add(distance):
            self.to_group(core, distance, self.group).wait_recv()
            self.offset[core] += self.total_in[core, distance - 1].astype(F32)

        self.groups_earlier(add)
        self.back[core] = (self.offset[core][None] + self.part[core]).astype(BF16)
        if self.backward:
            self.in_order(lambda member: self.to_member(core, member).start())
        else:
            self.far_first(lambda member: self.to_member(core, member).start(), planes=slice(0, 2))

    def receive(self):
        def wait(count):
            wait_bytes(self.back.at[0, pl.ds(0, count)], self.r3)

        self.by_core(lambda: wait(self.size), lambda: wait(self.size - 1))

    def drain(self):
        def sent(count):
            wait_bytes(self.inbox.at[0, pl.ds(0, count)], self.s1)

        def owner_sent():
            sent(self.size - 1)
            for core in range(CORES):
                self.groups_later(lambda distance, group: self.to_group(core, distance, group).wait_send())
                wait_bytes(self.back.at[core, pl.ds(0, self.size - (core == CORES - 1))], self.s3.at[core])

        self.by_core(lambda: sent(self.size), owner_sent)


def kernel(n_seq, n_head, size, *refs):
    q_hbm, k_hbm, v_hbm, cot_hbm, gain_hbm, gq, gk, gv = refs[:8]
    q, k, v, cot, gain, cot_block, scaled, inner, scores_t, query_t = refs[8:18]
    attended, grad, key_part, value_part, stat, stat_in = refs[18:24]
    local_sems, cot_send, cot_recv, stat_send, stat_recv = refs[24:29]
    scan_refs = [refs[at : at + 14] for at in range(29, 29 + 14 * 2 * HALVES, 14)]

    seq, head = lax.axis_index("seq"), lax.axis_index("head")
    groups = n_seq // size
    group, me = seq // size, lax.rem(seq, size)
    tokens, width = q.shape
    heads = width // DH
    cot_rows = cot.shape[0]
    scaling = DH ** (-0.5)
    place = (seq, head, group, me, size, groups)
    scans = [Scan(place, i >= HALVES, *own[:8], own[8:]) for i, own in enumerate(scan_refs)]
    forward, backward = scans[:HALVES], scans[HALVES:]
    columns = [slice(h * DH, (h + 1) * DH) for h in range(heads)]
    part_heads = heads // HALVES
    halves = [range(i * part_heads, (i + 1) * part_heads) for i in range(HALVES)]

    loads = [
        pltpu.make_async_copy(src, dst, local_sems.at[i])
        for i, (src, dst) in enumerate(
            [(k_hbm, k), (v_hbm, v), (cot_hbm, cot), (q_hbm, q), (gain_hbm, gain)]
        )
    ]
    for load in loads[:2]:
        load.start()

    barrier = pltpu.get_barrier_semaphore()

    def greet(other_seq, other_head):
        pl.semaphore_signal(
            barrier, inc=1, device_id=(other_seq, other_head), device_id_type=MESH
        )

    def greet_owners():
        forward[0].far_first(lambda member: greet(group * size + member, head + 1))

    def greet_owned():
        for step in range(1, groups):
            other = lax.rem(group + step, groups)
            greet(other * size + forward[0].piece(forward[0].mine, other), head)
        forward[0].far_first(
            lambda member: greet(group * size + member, head),
            lambda member: greet(group * size + member, head - 1),
        )

    forward[0].by_core(greet_owners, greet_owned)
    for step in range(1, n_head):
        greet(seq, lax.rem(head + step, n_head))
    for load in loads[2:]:
        load.start()

    loads[0].wait()
    loads[1].wait()
    for i, half in enumerate(halves):
        for h in half:
            state = dot(k[:, columns[h]], v[:, columns[h]], 0, 0)
            forward[i].state[columns[h - half[0]], :] = state.astype(BF16)
        if i == 0:
            forward[0].by_core(
                lambda: pl.semaphore_wait(barrier, size - 1 + n_head - 1),
                lambda: pl.semaphore_wait(barrier, 2 * (size - 1) + groups - 1 + n_head - 1),
            )
        forward[i].send_state()

    def cot_columns(to):
        return pl.ds(pl.multiple_of(to * width, width), width)

    def cot_rows_of(owner):
        return cot_block.at[pl.ds(pl.multiple_of(owner * cot_rows, cot_rows), cot_rows)]

    def cot_copy(to, owner):
        return remote(
            cot.at[:, cot_columns(to)],
            cot_rows_of(owner),
            cot_send,
            cot_recv,
            seq,
            to,
        )

    def over_heads(body):
        for step in range(1, n_head):
            body(lax.rem(head + step, n_head))

    loads[2].wait()
    over_heads(lambda to: cot_copy(to, head).start())
    cot_rows_of(head)[...] = cot[:, cot_columns(head)]

    loads[3].wait()
    loads[4].wait()
    rows = lax.broadcasted_iota(jnp.int32, (tokens, tokens), 0)
    cols = lax.broadcasted_iota(jnp.int32, (tokens, tokens), 1)

    def own_block(some):
        for h in some:
            qh, kh, vh = (ref[:, columns[h]] for ref in (q, k, v))
            raw = dot(qh, kh, 1, 1) * scaling
            masked = jnp.where(rows >= cols, raw, 0.0).astype(BF16)
            inner[:, columns[h]] = dot(masked, vh, 1, 0)

    def turned(some):
        for h in some:
            qh, kh = q[:, columns[h]], k[:, columns[h]]
            raw = dot(kh, qh, 1, 1) * scaling
            scores_t[h] = jnp.where(cols >= rows, raw, 0.0).astype(BF16)
            query_t[h] = qh.T

    own_block(range(heads // 2))

    def each(scan, *steps):
        def owner():
            order = range(CORES)
            for step in steps:
                for core in reversed(order) if scan.backward else order:
                    step(scan, core)

        pl.when(scan.owns)(owner)

    each(forward[0], Scan.sum_up, Scan.add_up)
    own_block(range(heads // 2, heads))
    wait_bytes(cot.at[:, pl.ds(0, (n_head - 1) * width)], cot_recv)
    scaled[...] = cot_block[...].astype(F32) * gain[:, cot_columns(head)]

    each(forward[0], Scan.answer, Scan.near)

    turned(range(heads))

    squares = jnp.zeros((tokens, DH), F32)
    products = jnp.zeros((tokens, DH), F32)
    for i, half in enumerate(halves):
        forward[i].receive()
        for h in half:
            prefix = forward[i].out[columns[h - half[0]], :]
            outer = dot(q[:, columns[h]], prefix, 1, 0) * scaling
            rounded = (inner[:, columns[h]] + outer).astype(BF16)
            attended[:, columns[h]] = rounded
            wide = rounded.astype(F32)
            squares = squares + wide * wide
            products = products + wide * scaled[:, columns[h]]
    square_row = jnp.sum(squares.T, axis=0, keepdims=True)
    product_row = jnp.sum(products.T, axis=0, keepdims=True)
    stat_rows = lax.broadcasted_iota(jnp.int32, stat.shape, 0)
    stat[...] = jnp.where(stat_rows == 0, square_row, product_row)

    def stat_copy(to, owner):
        return remote(
            stat, stat_in.at[owner], stat_send, stat_recv, seq, to
        )

    over_heads(lambda to: stat_copy(to, head).start())
    stat_in[head] = stat[...]
    wait_bytes(stat_in.at[pl.ds(0, n_head - 1)], stat_recv)
    summed = jnp.sum(stat_in[...], axis=0) * (1.0 / (n_head * width))
    inverse = lax.rsqrt(summed[0:1, :] + EPSILON)
    slope = inverse * inverse * inverse * summed[1:2, :]
    inverse = jnp.broadcast_to(inverse, (DH, tokens)).T
    slope = jnp.broadcast_to(slope, (DH, tokens)).T

    for i, half in enumerate(halves):
        for h in half:
            wide = attended[:, columns[h]].astype(F32)
            rounded = (inverse * scaled[:, columns[h]] - slope * wide).astype(BF16)
            grad[:, columns[h]] = rounded
            state = dot(query_t[h], rounded, 1, 0)
            backward[i].state[columns[h - half[0]], :] = state.astype(BF16)
        backward[i].send_state()

    def own_grads(h):
        at = columns[h]
        prefix = forward[h // part_heads].out[columns[h % part_heads], :]
        gh, qh, kh, vh = (ref[:, at] for ref in (grad, q, k, v))
        raw = dot(gh, vh, 1, 1) * scaling
        masked = jnp.where(rows >= cols, raw, 0.0).astype(BF16)
        raw = dot(vh, gh, 1, 1) * scaling
        masked_t = jnp.where(cols >= rows, raw, 0.0).astype(BF16)
        outer = dot(gh, prefix, 1, 1) * scaling
        gq[:, at] = (dot(masked, kh, 1, 0) + outer).astype(BF16)
        key_part[:, at] = dot(masked_t, qh, 1, 0)
        value_part[:, at] = dot(scores_t[h], gh, 1, 0)

    for h in range(heads - 2):
        own_grads(h)
    each(backward[0], Scan.sum_up, Scan.add_up)
    own_grads(heads - 2)
    each(backward[0], Scan.answer, Scan.near)
    own_grads(heads - 1)
    for i, half in enumerate(halves):
        backward[i].receive()
        for h in half:
            suffix = backward[i].out[columns[h - half[0]], :]
            outer = dot(v[:, columns[h]], suffix, 1, 1) * scaling
            gk[:, columns[h]] = (key_part[:, columns[h]] + outer).astype(BF16)
            outer = dot(k[:, columns[h]], suffix, 1, 0) * scaling
            gv[:, columns[h]] = (value_part[:, columns[h]] + outer).astype(BF16)

    for scan in scans:
        scan.drain()
    wait_bytes(cot.at[:, pl.ds(0, (n_head - 1) * width)], cot_send)
    wait_bytes(stat_in.at[pl.ds(0, n_head - 1)], stat_send)


def write_out(*refs):
    copies = [pltpu.make_async_copy(refs[i], refs[3 + i], refs[6].at[i]) for i in range(3)]
    for copy in copies:
        copy.start()
    for copy in copies:
        copy.wait()


def solution(mesh):
    n_seq, n_head = mesh.shape["seq"], mesh.shape["head"]
    size = GROUP
    groups = n_seq // size

    def local(queries, key_rows, values, cotangent, norm_gain):
        tokens, width = queries.shape
        heads = width // DH
        part = heads * DH // HALVES
        rows = part // size
        block = pltpu.VMEM((tokens, width), BF16)
        wide = pltpu.VMEM((tokens, width), F32)
        square = pltpu.VMEM((heads, DH, DH), BF16)
        scan = [
            pltpu.VMEM((part, DH), BF16),
            pltpu.VMEM((CORES, size, rows, DH), BF16),
            pltpu.VMEM((CORES, size, rows, DH), F32),
            pltpu.VMEM((CORES, rows, DH), BF16),
            pltpu.VMEM((CORES, groups - 1, rows, DH), BF16),
            pltpu.VMEM((CORES, rows, DH), F32),
            pltpu.VMEM((CORES, size, rows, DH), BF16),
            pltpu.VMEM((part, DH), BF16),
        ]
        dma = pltpu.SemaphoreType.DMA
        scan_sems = [dma, dma((CORES,))] + [dma((CORES, groups - 1))] * 2 + [dma((CORES,)), dma]
        out = pltpu.VMEM((tokens, width), BF16)
        grads = pl.pallas_call(
            functools.partial(kernel, n_seq, n_head, size),
            out_shape=(out, out, out),
            in_specs=[pl.BlockSpec(memory_space=pltpu.HBM)] * 5,
            out_specs=[pl.BlockSpec(memory_space=pltpu.VMEM)] * 3,
            scratch_shapes=[
                block,
                block,
                block,
                pltpu.VMEM(cotangent.shape, BF16),
                pltpu.VMEM((1, norm_gain.shape[0]), F32),
                block,
                wide,
                wide,
                square,
                square,
                block,
                block,
                wide,
                wide,
                pltpu.VMEM((8, tokens), F32),
                pltpu.VMEM((n_head, 8, tokens), F32),
                dma((5,)),
                dma,
                dma,
                dma,
                dma,
                *((scan + scan_sems) * (2 * HALVES)),
            ],
            compiler_params=pltpu.CompilerParams(
                collective_id=0, has_side_effects=True, vmem_limit_bytes=60 * 1024 * 1024
            ),
            cost_estimate=pl.CostEstimate(
                flops=26 * heads * DH**3, bytes_accessed=14 * tokens * width, transcendentals=0
            ),
        )(queries, key_rows, values, cotangent, norm_gain.reshape(1, -1))
        result = jax.ShapeDtypeStruct((tokens, width), BF16)
        return pl.pallas_call(
            write_out,
            out_shape=(result,) * 3,
            in_specs=[pl.BlockSpec(memory_space=pltpu.VMEM)] * 3,
            out_specs=[pl.BlockSpec(memory_space=pltpu.HBM)] * 3,
            scratch_shapes=[dma((3,))],
            compiler_params=pltpu.CompilerParams(vmem_limit_bytes=2 * 1024 * 1024),
        )(*grads)

    return jax.shard_map(
        local,
        mesh=mesh,
        in_specs=(P("seq", "head"), P("seq", "head"), P("seq", "head"), P(("seq", "head"), None), P()),
        out_specs=(P("seq", "head"), P("seq", "head"), P("seq", "head")),
        check_vma=False,
    )
```

```python
import functools

import jax
import jax.numpy as jnp
from jax import lax
from jax.experimental import pallas as pl
from jax.experimental.pallas import tpu as pltpu
from jax.sharding import PartitionSpec as P

DH = 128
EPSILON = 1e-06
GROUP = 16
HALVES = 1
CORES = 2
MESH = pl.DeviceIdType.MESH
F32 = jnp.float32
BF16 = jnp.bfloat16


def dot(left, right, left_dim, right_dim):
    dims = (((left_dim,), (right_dim,)), ((), ()))
    return lax.dot_general(left, right, dims, preferred_element_type=F32)


def remote(src, dst, send_sem, recv_sem, seq, head):
    return pltpu.make_async_remote_copy(
        src_ref=src,
        dst_ref=dst,
        send_sem=send_sem,
        recv_sem=recv_sem,
        device_id=(seq, head),
        device_id_type=MESH,
    )


def wait_bytes(ref, sem):
    pltpu.make_async_copy(ref, ref, sem).wait()


class Scan:
    def __init__(self, place, backward, state, inbox, part, total, total_in, offset, back, out, sems):
        self.seq, self.head, self.group, self.me, self.size, self.groups = place
        self.backward = backward
        self.state, self.inbox, self.part, self.total = state, inbox, part, total
        self.total_in, self.offset, self.back, self.out = total_in, offset, back, out
        self.s1, self.r1, self.s2, self.r2, self.s3, self.r3 = sems
        self.rows = inbox.shape[2]
        self.core = lax.rem(self.head, CORES)
        self.owner_head = self.head - self.core + CORES - 1
        self.owns = self.core == CORES - 1
        self.row = self.size // 4
        self.mine = self.piece(self.me, self.group)

    def slice_of(self, ref, owner):
        return ref.at[pl.ds(pl.multiple_of(owner * self.rows, self.rows), self.rows)]

    def piece(self, member, group):
        shifted = lax.rem((group + 1) // 2, 2)
        return lax.rem(member + shifted * (self.size // 2), self.size)

    def far_first(self, *bodies, planes=slice(None)):
        here, column = self.me // self.row, lax.rem(self.me, self.row)
        rows = self.size // self.row
        others = (rows - 1 - here, lax.rem(here + 2, rows), here + 1 - 2 * lax.rem(here, 2), here)
        for other in others[planes]:
            for step in range(1, self.row + (other is not here)):
                for body in bodies:
                    body(other * self.row + lax.rem(column + step, self.row))

    def to_owner(self, owner):
        return remote(
            self.slice_of(self.state, self.piece(owner, self.group)),
            self.inbox.at[self.core, self.me],
            self.s1,
            self.r1.at[self.core],
            self.group * self.size + owner,
            self.owner_head,
        )

    def to_group(self, core, distance, group):
        return remote(
            self.total.at[core],
            self.total_in.at[core, distance - 1],
            self.s2.at[core, distance - 1],
            self.r2.at[core, distance - 1],
            group * self.size + self.piece(self.mine, group),
            self.head,
        )

    def to_member(self, core, member):
        return remote(
            self.back.at[core, member],
            self.slice_of(self.out, self.mine),
            self.s3.at[core],
            self.r3,
            self.group * self.size + member,
            self.head - (CORES - 1) + core,
        )

    def groups_later(self, body):
        for distance in range(1, self.groups):
            if self.backward:
                group, there = self.group - distance, self.group >= distance
            else:
                group, there = self.group + distance, self.group + distance < self.groups
            pl.when(there)(functools.partial(body, distance, group))

    def groups_earlier(self, body):
        for distance in range(1, self.groups):
            if self.backward:
                there = self.group + distance < self.groups
            else:
                there = self.group >= distance
            pl.when(there)(functools.partial(body, distance))

    def by_core(self, first, second):
        pl.when(self.core != CORES - 1)(first)
        pl.when(self.owns)(second)

    def send_state(self):
        far, near = slice(None), slice(None, None, -1)

        def send(planes):
            self.far_first(lambda owner: self.to_owner(owner).start(), planes=planes)

        def first():
            send(near if self.backward else far)
            self.to_owner(self.me).start()

        def second():
            send(far if self.backward else near)
            self.inbox[CORES - 1, self.me] = self.slice_of(self.state, self.mine)[...]

        self.by_core(first, second)

    def sum_up(self, core):
        received = self.size - (core == CORES - 1)
        wait_bytes(self.inbox.at[core, pl.ds(0, received)], self.r1.at[core])
        total = jnp.zeros(self.offset.shape[1:], F32)
        for member in range(self.size):
            total = total + self.inbox[core, member].astype(F32)
        self.total[core] = total.astype(BF16)
        self.groups_later(lambda distance, group: self.to_group(core, distance, group).start())
        self.offset[core] = jnp.zeros(self.offset.shape[1:], F32)

    def add_up(self, core):
        running = jnp.zeros(self.offset.shape[1:], F32)
        order = range(self.size)
        for member in reversed(order) if self.backward else order:
            self.part[core, member] = running
            running = running + self.inbox[core, member].astype(F32)

    def in_order(self, body):
        here, column = self.me // self.row, lax.rem(self.me, self.row)
        for other in range(self.size // self.row):
            pl.when(here != other)(functools.partial(body, other * self.row + column))
            for step in range(1, self.row):
                body(other * self.row + lax.rem(column + step, self.row))

    def near(self, core):
        if not self.backward:
            self.far_first(lambda member: self.to_member(core, member).start(), planes=slice(2 - 2 * core, 4 - 2 * core))
        if core == CORES - 1:
            self.slice_of(self.out, self.mine)[...] = self.back[core, self.me]
        else:
            self.to_member(core, self.me).start()

    def answer(self, core):
        def add(distance):
            self.to_group(core, distance, self.group).wait_recv()
            self.offset[core] += self.total_in[core, distance - 1].astype(F32)

        self.groups_earlier(add)
        self.back[core] = (self.offset[core][None] + self.part[core]).astype(BF16)
        if self.backward:
            self.in_order(lambda member: self.to_member(core, member).start())
        else:
            self.far_first(lambda member: self.to_member(core, member).start(), planes=slice(2 * core, 2 + 2 * core))

    def receive(self):
        def wait(count):
            wait_bytes(self.back.at[0, pl.ds(0, count)], self.r3)

        self.by_core(lambda: wait(self.size), lambda: wait(self.size - 1))

    def drain(self):
        def sent(count):
            wait_bytes(self.inbox.at[0, pl.ds(0, count)], self.s1)

        def owner_sent():
            sent(self.size - 1)
            for core in range(CORES):
                self.groups_later(lambda distance, group: self.to_group(core, distance, group).wait_send())
                wait_bytes(self.back.at[core, pl.ds(0, self.size - (core == CORES - 1))], self.s3.at[core])

        self.by_core(lambda: sent(self.size), owner_sent)


def kernel(n_seq, n_head, size, *refs):
    q_hbm, k_hbm, v_hbm, cot_hbm, gain_hbm, gq, gk, gv = refs[:8]
    q, k, v, cot, gain, cot_block, scaled, inner, scores_t, query_t = refs[8:18]
    attended, grad, key_part, value_part, stat, stat_in = refs[18:24]
    local_sems, cot_send, cot_recv, stat_send, stat_recv = refs[24:29]
    scan_refs = [refs[at : at + 14] for at in range(29, 29 + 14 * 2 * HALVES, 14)]

    seq, head = lax.axis_index("seq"), lax.axis_index("head")
    groups = n_seq // size
    group, me = seq // size, lax.rem(seq, size)
    tokens, width = q.shape
    heads = width // DH
    cot_rows = cot.shape[0]
    scaling = DH ** (-0.5)
    place = (seq, head, group, me, size, groups)
    scans = [Scan(place, i >= HALVES, *own[:8], own[8:]) for i, own in enumerate(scan_refs)]
    forward, backward = scans[:HALVES], scans[HALVES:]
    columns = [slice(h * DH, (h + 1) * DH) for h in range(heads)]
    part_heads = heads // HALVES
    halves = [range(i * part_heads, (i + 1) * part_heads) for i in range(HALVES)]

    loads = [
        pltpu.make_async_copy(src, dst, local_sems.at[i])
        for i, (src, dst) in enumerate(
            [(k_hbm, k), (v_hbm, v), (cot_hbm, cot), (q_hbm, q), (gain_hbm, gain)]
        )
    ]
    for load in loads[:2]:
        load.start()

    barrier = pltpu.get_barrier_semaphore()

    def greet(other_seq, other_head):
        pl.semaphore_signal(
            barrier, inc=1, device_id=(other_seq, other_head), device_id_type=MESH
        )

    def greet_owners():
        forward[0].far_first(lambda member: greet(group * size + member, head + 1))

    def greet_owned():
        for step in range(1, groups):
            other = lax.rem(group + step, groups)
            greet(other * size + forward[0].piece(forward[0].mine, other), head)
        forward[0].far_first(
            lambda member: greet(group * size + member, head),
            lambda member: greet(group * size + member, head - 1),
        )

    forward[0].by_core(greet_owners, greet_owned)
    for step in range(1, n_head):
        greet(seq, lax.rem(head + step, n_head))
    for load in loads[2:]:
        load.start()

    loads[0].wait()
    loads[1].wait()
    for i, half in enumerate(halves):
        for h in half:
            state = dot(k[:, columns[h]], v[:, columns[h]], 0, 0)
            forward[i].state[columns[h - half[0]], :] = state.astype(BF16)
        if i == 0:
            forward[0].by_core(
                lambda: pl.semaphore_wait(barrier, size - 1 + n_head - 1),
                lambda: pl.semaphore_wait(barrier, 2 * (size - 1) + groups - 1 + n_head - 1),
            )
        forward[i].send_state()

    def cot_columns(to):
        return pl.ds(pl.multiple_of(to * width, width), width)

    def cot_rows_of(owner):
        return cot_block.at[pl.ds(pl.multiple_of(owner * cot_rows, cot_rows), cot_rows)]

    def cot_copy(to, owner):
        return remote(
            cot.at[:, cot_columns(to)],
            cot_rows_of(owner),
            cot_send,
            cot_recv,
            seq,
            to,
        )

    def over_heads(body):
        for step in range(1, n_head):
            body(lax.rem(head + step, n_head))

    loads[2].wait()
    over_heads(lambda to: cot_copy(to, head).start())
    cot_rows_of(head)[...] = cot[:, cot_columns(head)]

    loads[3].wait()
    loads[4].wait()
    rows = lax.broadcasted_iota(jnp.int32, (tokens, tokens), 0)
    cols = lax.broadcasted_iota(jnp.int32, (tokens, tokens), 1)

    def own_block(some):
        for h in some:
            qh, kh, vh = (ref[:, columns[h]] for ref in (q, k, v))
            raw = dot(qh, kh, 1, 1) * scaling
            masked = jnp.where(rows >= cols, raw, 0.0).astype(BF16)
            inner[:, columns[h]] = dot(masked, vh, 1, 0)

    def turned(some):
        for h in some:
            qh, kh = q[:, columns[h]], k[:, columns[h]]
            raw = dot(kh, qh, 1, 1) * scaling
            scores_t[h] = jnp.where(cols >= rows, raw, 0.0).astype(BF16)
            query_t[h] = qh.T

    own_block(range(heads // 2))

    def each(scan, *steps):
        def owner():
            order = range(CORES)
            for step in steps:
                for core in reversed(order) if scan.backward else order:
                    step(scan, core)

        pl.when(scan.owns)(owner)

    each(forward[0], Scan.sum_up, Scan.add_up)
    own_block(range(heads // 2, heads))
    wait_bytes(cot.at[:, pl.ds(0, (n_head - 1) * width)], cot_recv)
    scaled[...] = cot_block[...].astype(F32) * gain[:, cot_columns(head)]

    each(forward[0], Scan.answer, Scan.near)

    turned(range(heads))

    squares = jnp.zeros((tokens, DH), F32)
    products = jnp.zeros((tokens, DH), F32)
    for i, half in enumerate(halves):
        forward[i].receive()
        for h in half:
            prefix = forward[i].out[columns[h - half[0]], :]
            outer = dot(q[:, columns[h]], prefix, 1, 0) * scaling
            rounded = (inner[:, columns[h]] + outer).astype(BF16)
            attended[:, columns[h]] = rounded
            wide = rounded.astype(F32)
            squares = squares + wide * wide
            products = products + wide * scaled[:, columns[h]]
    square_row = jnp.sum(squares.T, axis=0, keepdims=True)
    product_row = jnp.sum(products.T, axis=0, keepdims=True)
    stat_rows = lax.broadcasted_iota(jnp.int32, stat.shape, 0)
    stat[...] = jnp.where(stat_rows == 0, square_row, product_row)

    def stat_copy(to, owner):
        return remote(
            stat, stat_in.at[owner], stat_send, stat_recv, seq, to
        )

    over_heads(lambda to: stat_copy(to, head).start())
    stat_in[head] = stat[...]
    wait_bytes(stat_in.at[pl.ds(0, n_head - 1)], stat_recv)
    summed = jnp.sum(stat_in[...], axis=0) * (1.0 / (n_head * width))
    inverse = lax.rsqrt(summed[0:1, :] + EPSILON)
    slope = inverse * inverse * inverse * summed[1:2, :]
    inverse = jnp.broadcast_to(inverse, (DH, tokens)).T
    slope = jnp.broadcast_to(slope, (DH, tokens)).T

    for i, half in enumerate(halves):
        for h in half:
            wide = attended[:, columns[h]].astype(F32)
            rounded = (inverse * scaled[:, columns[h]] - slope * wide).astype(BF16)
            grad[:, columns[h]] = rounded
            state = dot(query_t[h], rounded, 1, 0)
            backward[i].state[columns[h - half[0]], :] = state.astype(BF16)
        backward[i].send_state()

    def own_grads(h):
        at = columns[h]
        prefix = forward[h // part_heads].out[columns[h % part_heads], :]
        gh, qh, kh, vh = (ref[:, at] for ref in (grad, q, k, v))
        raw = dot(gh, vh, 1, 1) * scaling
        masked = jnp.where(rows >= cols, raw, 0.0).astype(BF16)
        raw = dot(vh, gh, 1, 1) * scaling
        masked_t = jnp.where(cols >= rows, raw, 0.0).astype(BF16)
        outer = dot(gh, prefix, 1, 1) * scaling
        gq[:, at] = (dot(masked, kh, 1, 0) + outer).astype(BF16)
        key_part[:, at] = dot(masked_t, qh, 1, 0)
        value_part[:, at] = dot(scores_t[h], gh, 1, 0)

    for h in range(heads - 2):
        own_grads(h)
    each(backward[0], Scan.sum_up, Scan.add_up)
    own_grads(heads - 2)
    each(backward[0], Scan.answer, Scan.near)
    own_grads(heads - 1)
    for i, half in enumerate(halves):
        backward[i].receive()
        for h in half:
            suffix = backward[i].out[columns[h - half[0]], :]
            outer = dot(v[:, columns[h]], suffix, 1, 1) * scaling
            gk[:, columns[h]] = (key_part[:, columns[h]] + outer).astype(BF16)
            outer = dot(k[:, columns[h]], suffix, 1, 0) * scaling
            gv[:, columns[h]] = (value_part[:, columns[h]] + outer).astype(BF16)

    for scan in scans:
        scan.drain()
    wait_bytes(cot.at[:, pl.ds(0, (n_head - 1) * width)], cot_send)
    wait_bytes(stat_in.at[pl.ds(0, n_head - 1)], stat_send)


def write_out(*refs):
    copies = [pltpu.make_async_copy(refs[i], refs[3 + i], refs[6].at[i]) for i in range(3)]
    for copy in copies:
        copy.start()
    for copy in copies:
        copy.wait()


def solution(mesh):
    n_seq, n_head = mesh.shape["seq"], mesh.shape["head"]
    size = GROUP
    groups = n_seq // size

    def local(queries, key_rows, values, cotangent, norm_gain):
        tokens, width = queries.shape
        heads = width // DH
        part = heads * DH // HALVES
        rows = part // size
        block = pltpu.VMEM((tokens, width), BF16)
        wide = pltpu.VMEM((tokens, width), F32)
        square = pltpu.VMEM((heads, DH, DH), BF16)
        scan = [
            pltpu.VMEM((part, DH), BF16),
            pltpu.VMEM((CORES, size, rows, DH), BF16),
            pltpu.VMEM((CORES, size, rows, DH), F32),
            pltpu.VMEM((CORES, rows, DH), BF16),
            pltpu.VMEM((CORES, groups - 1, rows, DH), BF16),
            pltpu.VMEM((CORES, rows, DH), F32),
            pltpu.VMEM((CORES, size, rows, DH), BF16),
            pltpu.VMEM((part, DH), BF16),
        ]
        dma = pltpu.SemaphoreType.DMA
        scan_sems = [dma, dma((CORES,))] + [dma((CORES, groups - 1))] * 2 + [dma((CORES,)), dma]
        out = pltpu.VMEM((tokens, width), BF16)
        grads = pl.pallas_call(
            functools.partial(kernel, n_seq, n_head, size),
            out_shape=(out, out, out),
            in_specs=[pl.BlockSpec(memory_space=pltpu.HBM)] * 5,
            out_specs=[pl.BlockSpec(memory_space=pltpu.VMEM)] * 3,
            scratch_shapes=[
                block,
                block,
                block,
                pltpu.VMEM(cotangent.shape, BF16),
                pltpu.VMEM((1, norm_gain.shape[0]), F32),
                block,
                wide,
                wide,
                square,
                square,
                block,
                block,
                wide,
                wide,
                pltpu.VMEM((8, tokens), F32),
                pltpu.VMEM((n_head, 8, tokens), F32),
                dma((5,)),
                dma,
                dma,
                dma,
                dma,
                *((scan + scan_sems) * (2 * HALVES)),
            ],
            compiler_params=pltpu.CompilerParams(
                collective_id=0, has_side_effects=True, vmem_limit_bytes=60 * 1024 * 1024
            ),
            cost_estimate=pl.CostEstimate(
                flops=26 * heads * DH**3, bytes_accessed=14 * tokens * width, transcendentals=0
            ),
        )(queries, key_rows, values, cotangent, norm_gain.reshape(1, -1))
        result = jax.ShapeDtypeStruct((tokens, width), BF16)
        return pl.pallas_call(
            write_out,
            out_shape=(result,) * 3,
            in_specs=[pl.BlockSpec(memory_space=pltpu.VMEM)] * 3,
            out_specs=[pl.BlockSpec(memory_space=pltpu.HBM)] * 3,
            scratch_shapes=[dma((3,))],
            compiler_params=pltpu.CompilerParams(vmem_limit_bytes=2 * 1024 * 1024),
        )(*grads)

    return jax.shard_map(
        local,
        mesh=mesh,
        in_specs=(P("seq", "head"), P("seq", "head"), P("seq", "head"), P(("seq", "head"), None), P()),
        out_specs=(P("seq", "head"), P("seq", "head"), P("seq", "head")),
        check_vma=False,
    )
```
